32 devices in a mesh: section: 4 (over z), dp: 8 (over y, x, core).
Axes of the slice: x: 2, y: 2, z: 4, core: 2. Of those that a mesh axis runs over, the one named last changes fastest.
Arguments:
- act_in: float32 [4, 2, 8, 15, 15, 256], P('section', None, 'dp'), may hold values from -6 to 6
- act_mid: float32 [4, 2, 8, 15, 15, 256], P('section', None, 'dp'), may hold values from 0 to 2
- relu_mask: int32 [4, 2, 8, 15, 15, 256], P('section', None, 'dp'), may hold values 0 or 1
- arriving: float32 [4, 8, 15, 15, 256], P('section', 'dp'), may hold values from -6 to 6
- loss_grad: float32 [1, 8, 15, 15, 256], P(None, 'dp'), may hold values from -6 to 6
- w_first: float32 [4, 1792, 256], P('section', 'dp'), may hold values from -0.125 to 0.125
- w_second: float32 [4, 1792, 256], P('section', 'dp'), may hold values from -0.125 to 0.125
Outputs:
- data_grad: float32 [4, 2, 8, 15, 15, 256], P('section', None, 'dp')
- first_grad: float32 [4, 1792, 256], P('section', 'dp')
- second_grad: float32 [4, 1792, 256], P('section', 'dp')
The draws below stay inside these ranges and needn't reach their ends.
All inputs are finite; a program needn't handle non-finite values. No bound on the sum of `relu_mask` on one device may be relied on, other than what follows from the above.
Results may differ from the reference program's by a relative error of at most 0.00011.
Values sent between devices are 32-bit elements; how exact they have to be, the bound alone decides.
No kernel may reach another device: no remote copies, remote signals or barrier semaphores. Data moves between devices by JAX's collectives and lax.ppermute only.
A program may use at most 64 MiB of HBM per device.

```python
import jax
import jax.numpy as jnp
from jax import lax

C = 256
HGT = 15
WID = 15
TICKS = 2
SECTIONS = 4
IMAGES = 8


def plant(entries, stream_key, low, high):
    longest = entries.shape.index(max(entries.shape))
    spots = []
    for shift in (0, 1):
        where = [jax.random.randint(jax.random.fold_in(stream_key, axis), (), 0, length) for axis, length in enumerate(entries.shape)]
        where[longest] = (where[longest] + shift) % entries.shape[longest]
        spots.append(tuple(where))
    return entries.at[spots[0]].set(low).at[spots[1]].set(high)


def spiked(drawn, own_key, source, target, blocks, factor):
    def block_of(position):
        return (jnp.arange(drawn.shape[position]) // (drawn.shape[position] // blocks)).reshape((-1,) + (1,) * (drawn.ndim - 1 - position))

    one_side = jax.random.permutation(own_key, blocks)[block_of(target)]
    other_side = (block_of(target) + blocks // 2) % blocks
    return jnp.where((block_of(source) == one_side) | (block_of(source) == other_side), factor * drawn, drawn)


def block_levels(rng, shape, shards, low, largest):
    def one(dim, shards_of):
        draws = jax.random.uniform(jax.random.fold_in(jax.random.fold_in(rng, 6), dim), (shards_of,), jnp.float32, low / len(shards), largest / len(shards))
        return jnp.repeat(jnp.exp(draws), shape[dim] // shards_of).reshape((-1,) + (1,) * (len(shape) - dim - 1))

    gain = one(*shards[0])
    for cut in shards[1:]:
        gain = gain * one(*cut)
    return gain


def normal_values(key, shape, width, bound, split=(), kind=jnp.bfloat16):
    array = jax.random.normal(key, shape, jnp.float32) * width
    if len(split) > 0:
        array = block_levels(key, shape, split, -0.22, 0.18) * array
    return jnp.clip(array, min=-bound, max=bound).astype(kind)


def bell_draw_with(stream_key, shape, deviation, limit, cuts, heavy, kind=jnp.bfloat16):
    array = deviation * jax.random.normal(stream_key, shape, jnp.float32)
    if cuts:
        array = array * block_levels(stream_key, shape, cuts, -0.22, 0.18)
    return jnp.clip(spiked(array, jax.random.fold_in(stream_key, 3), *heavy), -limit, limit).astype(kind)


def setup_inputs(seed: int = 0) -> dict:
    splits = jax.random.split(jax.random.key(seed), 8)
    act_in = bell_draw_with(splits[0], (SECTIONS, TICKS, IMAGES, HGT, WID, C), 1.0, 6.0, ((0, 4), (2, 8)), (2, 5, 8, 2.0), jnp.float32)
    act_mid = jnp.clip(2.0 * jax.random.uniform(splits[1], (SECTIONS, TICKS, IMAGES, HGT, WID, C), jnp.float32) ** block_levels(splits[1], (SECTIONS, TICKS, IMAGES, HGT, WID, C), ((0, 4), (2, 8)), -0.2, 0.2), 0.0, 2.0)
    relu_mask = plant((jax.random.randint(splits[2], (SECTIONS, TICKS, IMAGES, HGT, WID, C), 0, 2) < 1).astype(jnp.int32), jax.random.fold_in(splits[2], 1), 0, 1)
    arriving = normal_values(splits[3], (SECTIONS, IMAGES, HGT, WID, C), 1.0, 6.0, ((0, 4), (1, 8)), jnp.float32)
    loss_grad = normal_values(splits[4], (TICKS - 1, IMAGES, HGT, WID, C), 1.0, 6.0, ((1, 8),), jnp.float32)
    w_first = normal_values(splits[5], (SECTIONS, 7 * C, C), (7 * C) ** -0.5, 0.125, ((0, 4), (1, 8)), jnp.float32)
    w_second = normal_values(splits[6], (SECTIONS, 7 * C, C), (7 * C) ** -0.5, 0.125, ((0, 4), (1, 8)), jnp.float32)
    return dict(act_in=act_in, act_mid=act_mid, relu_mask=relu_mask, arriving=arriving, loss_grad=loss_grad, w_first=w_first, w_second=w_second)


def spread_taps(values, spatial):
    widths = [(0, 0)] * 4
    widths[spatial] = (3, 3)
    padded = jnp.pad(values, widths)
    extent = values.shape[spatial]
    pieces = [lax.slice_in_dim(padded, offset, offset + extent, axis=spatial) for offset in range(7)]
    return jnp.concatenate(pieces, axis=-1)


def fold_taps(products, spatial):
    channels = products.shape[-1] // 7
    widths = [(0, 0)] * 4
    widths[spatial] = (3, 3)
    padded = jnp.pad(products, widths)
    extent = products.shape[spatial]
    summed = jnp.zeros(products.shape[:-1] + (channels,), products.dtype)
    for offset in range(7):
        window = lax.slice_in_dim(padded, 6 - offset, 6 - offset + extent, axis=spatial)
        summed = summed + window[..., offset * channels:(offset + 1) * channels]
    return summed


def project_taps(values, weight):
    return jnp.einsum("nhwc,kc->nhwk", values, weight, precision=lax.Precision.HIGHEST)


def section_backward(incoming, relu_mask, w_first, w_second):
    mid_grad = fold_taps(project_taps(incoming, w_second), 1)
    pre_grad = mid_grad * relu_mask.astype(jnp.float32)
    data_grad = fold_taps(project_taps(pre_grad, w_first), 2)
    return data_grad, pre_grad


def replica_sum(activations, grad_rows, spatial, mean_scale):
    tick_count, images = activations.shape[:2]
    patches = spread_taps(activations.reshape((tick_count * images,) + activations.shape[2:]), spatial)
    grouped = grad_rows.reshape((tick_count * images,) + grad_rows.shape[2:])
    return jnp.einsum("nhwk,nhwc->kc", patches, grouped, precision=lax.Precision.HIGHEST) * mean_scale


def reference(act_in, act_mid, relu_mask, arriving, loss_grad, w_first, w_second):
    tick_count = act_in.shape[1]
    incoming = arriving
    in_list, pre_list, out_list = [], [], []
    for tick_index in range(tick_count):
        if tick_index > 0:
            incoming = jnp.concatenate([out_list[-1][1:], loss_grad[tick_index - 1][None]], axis=0)
        outgoing, pre_grad = lax.map(lambda packed: section_backward(*packed),
                                     (incoming, relu_mask[:, tick_index], w_first, w_second))
        in_list.append(incoming)
        pre_list.append(pre_grad)
        out_list.append(outgoing)
    data_grad = jnp.stack(out_list, axis=1)
    incoming_all = jnp.stack(in_list, axis=1)
    pre_all = jnp.stack(pre_list, axis=1)
    mean_scale = 1.0 / (tick_count * act_in.shape[2])

    def filter_grads(packed):
        inputs_section, mids_section, incoming_section, pre_section = packed
        first_part = replica_sum(inputs_section, pre_section, 2, mean_scale)
        second_part = replica_sum(mids_section, incoming_section, 1, mean_scale)
        return first_part, second_part

    first_grad, second_grad = lax.map(filter_grads, (act_in, act_mid, incoming_all, pre_all))
    return data_grad, first_grad, second_grad
```

```python
import functools

import jax
import jax.numpy as jnp
from jax import lax
from jax.experimental import pallas as pl
from jax.experimental.pallas import tpu as pltpu
from jax.sharding import PartitionSpec as P

TAPS = 7
REACH = TAPS // 2
GROUP = 16
LANES = 128
F32 = jnp.float32
BF16 = jnp.bfloat16
NT = (((1,), (1,)), ((), ()))
NN = (((1,), (0,)), ((), ()))
VMEM = pl.BlockSpec(memory_space=pltpu.VMEM)
SMEM = pl.BlockSpec(memory_space=pltpu.SMEM)


def call(kernel, out_shapes, scratch, flops, *operands, scalars=0):
    moved = sum(x.size * x.dtype.itemsize for x in operands)
    moved += sum(s.size * s.dtype.itemsize for s in out_shapes)
    return pl.pallas_call(
        kernel,
        out_shape=out_shapes,
        in_specs=[SMEM] * scalars + [VMEM] * (len(operands) - scalars),
        out_specs=[VMEM] * len(out_shapes),
        scratch_shapes=scratch,
        compiler_params=pltpu.CompilerParams(vmem_limit_bytes=40 * 1024 * 1024),
        cost_estimate=pl.CostEstimate(flops=flops, bytes_accessed=moved, transcendentals=0),
    )(*operands)


def split(value):
    high = value.astype(BF16)
    return high, (value - high.astype(F32)).astype(BF16)


def padded_rows(rows):
    return rows + 2 * REACH * GROUP


def fill(rows_ref, high_ref, low_ref):
    rows, channels = rows_ref.shape
    edge = REACH * GROUP
    border = jnp.zeros((edge, channels), BF16)
    high, low = split(rows_ref[...])
    for ref, body in ((high_ref, high), (low_ref, low)):
        ref[pl.ds(0, edge), :] = border
        ref[pl.ds(edge, rows), :] = body
        ref[pl.ds(edge + rows, edge), :] = border


def dot(a, b, dims):
    return lax.dot_general(a, b, dims, preferred_element_type=F32)


def window(ref, tap, rows):
    return ref[pl.ds((TAPS - 1 - tap) * GROUP, rows), :]


def convolve(high_ref, low_ref, w_high, w_low, rows):
    channels = w_high.shape[0] // TAPS
    total = jnp.zeros((rows, channels), F32)
    for tap in range(TAPS):
        taken = pl.ds(tap * channels, channels)
        high, low = window(high_ref, tap, rows), window(low_ref, tap, rows)
        total += dot(high, w_high[taken, :], NT)
        total += dot(low, w_high[taken, :], NT)
        total += dot(high, w_low[taken, :], NT)
    return total


def regroup(source_ref, out_ref, groups, members):
    tail = jnp.zeros((GROUP - groups, out_ref.shape[-1]), F32)
    for member in range(members):
        for lane in range(source_ref.shape[0]):
            taken = source_ref[lane, pl.ds(member, groups, stride=GROUP), :]
            out_ref[pl.ds(member * GROUP, groups), lane * LANES : (lane + 1) * LANES] = taken
        out_ref[pl.ds(member * GROUP + groups, GROUP - groups), :] = tail


def place(starts_ref, pieces, w_high, w_low):
    for index, piece in enumerate(pieces):
        high, low = split(piece[...])
        taken = pl.ds(pl.multiple_of(starts_ref[index], GROUP), piece.shape[0])
        w_high[taken, :] = high
        w_low[taken, :] = low


def conv_kernel(piece_count, masked, members, *refs):
    refs = list(refs)
    if piece_count:
        starts = refs.pop(0)
    rows_ref = refs.pop(0)
    mask_ref = refs.pop(0) if masked else None
    if piece_count:
        pieces = [refs.pop(0) for _ in range(piece_count)]
        out_ref, w_high, w_low, high, low, flat = refs
        place(starts, pieces, w_high, w_low)
    else:
        w_high, w_low, out_ref, high, low, flat = refs
    rows = rows_ref.shape[0]
    fill(rows_ref, high, low)
    total = convolve(high, low, w_high, w_low, rows)
    if masked:
        total = total * mask_ref[...].astype(F32)
    for lane in range(flat.shape[0]):
        flat[lane] = total[:, lane * LANES : (lane + 1) * LANES]
    regroup(flat, out_ref, rows // GROUP, members)


def conv(rows, mask, members, weights=None, pieces=None):
    count, channels = rows.shape
    filter_rows = TAPS * channels
    out = [jax.ShapeDtypeStruct((members * GROUP, channels), F32)]
    operands, scalars = [rows], 0
    if mask is not None:
        operands.append(mask)
    if pieces is not None:
        starts, parts = pieces
        out += [jax.ShapeDtypeStruct((filter_rows, channels), BF16)] * 2
        operands = [starts] + operands + parts
        scalars = 1
    else:
        operands += weights
    scratch = [
        pltpu.VMEM((padded_rows(count), channels), BF16),
        pltpu.VMEM((padded_rows(count), channels), BF16),
        pltpu.VMEM((channels // LANES, count, LANES), F32),
    ]
    piece_count = 0 if pieces is None else len(pieces[1])
    kernel = functools.partial(conv_kernel, piece_count, mask is not None, members)
    result = call(kernel, out, scratch, 6 * count * filter_rows * channels, *operands, scalars=scalars)
    return result if pieces is not None else result[0]


def turn_kernel(in_ref, mid_ref, *outs):
    for ref, high, low in ((in_ref, outs[0], outs[1]), (mid_ref, outs[2], outs[3])):
        for tick in range(ref.shape[0]):
            taken_high, taken_low = split(ref[tick].T)
            high[tick] = taken_high
            low[tick] = taken_low


def turned(act_in, act_mid):
    out = []
    for act in (act_in, act_mid):
        out += [jax.ShapeDtypeStruct((act.shape[0], act.shape[2], act.shape[1]), BF16)] * 2
    return call(turn_kernel, out, [], 0, act_in, act_mid)


def correlate_kernel(scale, carried, *refs):
    if carried:
        act_high, act_low, rows_ref, before, out_ref, high, low = refs
    else:
        act_high, act_low, rows_ref, out_ref, high, low = refs
    fill(rows_ref, high, low)
    rows, channels = rows_ref.shape
    for tap in range(TAPS):
        taken = pl.ds(tap * channels, channels)
        here_high, here_low = window(high, tap, rows), window(low, tap, rows)
        total = dot(act_high[...], here_high, NN)
        total += dot(act_low[...], here_high, NN)
        total += dot(act_high[...], here_low, NN)
        total *= scale
        if carried:
            total += before[taken, :]
        out_ref[taken, :] = total


def correlate(act_high, act_low, rows, scale, before=None):
    count, channels = rows.shape
    out = [jax.ShapeDtypeStruct((TAPS * channels, channels), F32)]
    scratch = [pltpu.VMEM((padded_rows(count), channels), BF16)] * 2
    operands = [act_high, act_low, rows] + ([] if before is None else [before])
    kernel = functools.partial(correlate_kernel, scale, before is not None)
    return call(kernel, out, scratch, 6 * count * TAPS * channels * channels, *operands)[0]


def by_row(values):
    spare = GROUP - values.shape[-2]
    values = jnp.pad(values, [(0, 0)] * (values.ndim - 2) + [(0, spare), (0, 0)])
    return values.reshape(values.shape[:-3] + (-1, values.shape[-1]))


def by_column(values):
    return by_row(jnp.swapaxes(values, -3, -2))


def swap(shard, bit):
    peers = lax.axis_size("dp")
    return lax.ppermute(shard, "dp", [(i, i ^ bit) for i in range(peers)])


def four_chips():
    return lax.axis_size("dp") == 8


def gather(shards):
    if not four_chips():
        wholes = [lax.all_gather(shard, "dp", axis=0, tiled=True) for shard in shards]
        return [(jnp.zeros((1,), jnp.int32), [whole]) for whole in wholes]
    me = lax.axis_index("dp")
    first = [(swap(shard, 2), swap(shard, 4)) for shard in shards]
    result = []
    for shard, (by_x, by_y) in zip(shards, first):
        rows = shard.shape[0]
        half = rows // 2
        far_a = swap(by_x[:half], 4)
        far_b = swap(by_y[half:], 2)
        own = [(shard, 0, 0), (by_x, 2, 0), (by_y, 4, 0), (far_a, 6, 0), (far_b, 6, half)]
        pieces = own + [(swap(piece, 1), bits ^ 1, offset) for piece, bits, offset in own]
        starts = jnp.stack([(me ^ bits) * rows + offset for _, bits, offset in pieces])
        result.append((starts.astype(jnp.int32), [piece for piece, _, _ in pieces]))
    return result


def scatter(partial):
    if not four_chips():
        return lax.psum_scatter(partial, "dp", scatter_dimension=0, tiled=True)
    me = lax.axis_index("dp")
    rows = partial.shape[0] // 8
    half = rows // 2

    def block(bits):
        return lax.dynamic_slice_in_dim(partial, (me ^ bits) * rows, rows, axis=0)

    sent = swap(jnp.stack([block(bits) for bits in (1, 3, 5, 7)]), 1)
    kept = jnp.stack([block(bits) for bits in (0, 2, 4, 6)])
    chip = kept + sent
    a, b = chip[:, :half], chip[:, half:]
    a_there = swap(jnp.stack([a[1], a[3]]), 2)
    b_there = swap(jnp.stack([b[2], b[3]]), 4)
    a_near, a_far = a[0] + a_there[0], a[2] + a_there[1]
    b_near, b_far = b[0] + b_there[0], b[1] + b_there[1]
    a_last = swap(a_far, 4)
    b_last = swap(b_far, 2)
    return jnp.concatenate([a_near + a_last, b_near + b_last], axis=0)


def local(act_in, act_mid, relu_mask, arriving, loss_grad, w_first, w_second):
    ticks, images, height, width = act_in.shape[1:5]
    sections = lax.axis_size("section")
    is_last = lax.axis_index("section") == sections - 1
    scale = 1.0 / (ticks * images * lax.axis_size("dp"))
    second_pieces, first_pieces = gather([w_second[0], w_first[0]])
    in_high, in_low, mid_high, mid_low = turned(by_column(act_in[0, :, 0]), by_row(act_mid[0, :, 0]))
    mask = by_row(relu_mask[0, :, 0])
    loss = by_row(loss_grad[:, 0])
    incoming = by_row(arriving[0, 0])
    second = correlate(mid_high[0], mid_low[0], incoming, scale)
    pre, *w_second_parts = conv(incoming, mask[0], width, pieces=second_pieces)
    out, *w_first_parts = conv(pre, None, height, pieces=first_pieces)
    outs = [out]
    first = correlate(in_high[0], in_low[0], pre, scale)
    for tick in range(1, ticks):
        pairs = [(i, i - 1) for i in range(1, sections)]
        above = lax.ppermute(outs[-1], "section", pairs)
        incoming = jnp.where(is_last, loss[tick - 1], above)
        second = correlate(mid_high[tick], mid_low[tick], incoming, scale, second)
        pre = conv(incoming, mask[tick], width, weights=w_second_parts)
        first = correlate(in_high[tick], in_low[tick], pre, scale, first)
        outs.append(conv(pre, None, height, weights=w_first_parts))
    second_grad = scatter(second)
    first_grad = scatter(first)
    data_grad = jnp.stack(outs).reshape(ticks, height, GROUP, -1)[:, :, :width]
    return data_grad[None, :, None], first_grad[None], second_grad[None]


def solution(mesh):
    return jax.shard_map(
        local,
        mesh=mesh,
        in_specs=(
            P("section", None, "dp", None, None, None),
            P("section", None, "dp", None, None, None),
            P("section", None, "dp", None, None, None),
            P("section", "dp", None, None, None),
            P(None, "dp", None, None, None),
            P("section", "dp", None),
            P("section", "dp", None),
        ),
        out_specs=(
            P("section", None, "dp", None, None, None),
            P("section", "dp", None),
            P("section", "dp", None),
        ),
        check_vma=False,
    )
```

```python
import functools

import jax
import jax.numpy as jnp
from jax import lax
from jax.experimental import pallas as pl
from jax.experimental.pallas import tpu as pltpu
from jax.sharding import PartitionSpec as P

TAPS = 7
REACH = TAPS // 2
GROUP = 16
LANES = 128
F32 = jnp.float32
BF16 = jnp.bfloat16
NT = (((1,), (1,)), ((), ()))
NN = (((1,), (0,)), ((), ()))
VMEM = pl.BlockSpec(memory_space=pltpu.VMEM)
SMEM = pl.BlockSpec(memory_space=pltpu.SMEM)


def call(kernel, out_shapes, scratch, flops, *operands, scalars=0):
    moved = sum(x.size * x.dtype.itemsize for x in operands)
    moved += sum(s.size * s.dtype.itemsize for s in out_shapes)
    return pl.pallas_call(
        kernel,
        out_shape=out_shapes,
        in_specs=[SMEM] * scalars + [VMEM] * (len(operands) - scalars),
        out_specs=[VMEM] * len(out_shapes),
        scratch_shapes=scratch,
        compiler_params=pltpu.CompilerParams(vmem_limit_bytes=40 * 1024 * 1024),
        cost_estimate=pl.CostEstimate(flops=flops, bytes_accessed=moved, transcendentals=0),
    )(*operands)


def split(value):
    high = value.astype(BF16)
    return high, (value - high.astype(F32)).astype(BF16)


def padded_rows(rows):
    return rows + 2 * REACH * GROUP


def fill(rows_ref, high_ref, low_ref):
    rows, channels = rows_ref.shape
    edge = REACH * GROUP
    border = jnp.zeros((edge, channels), BF16)
    high, low = split(rows_ref[...])
    for ref, body in ((high_ref, high), (low_ref, low)):
        ref[pl.ds(0, edge), :] = border
        ref[pl.ds(edge, rows), :] = body
        ref[pl.ds(edge + rows, edge), :] = border


def dot(a, b, dims):
    return lax.dot_general(a, b, dims, preferred_element_type=F32)


def window(ref, tap, rows):
    return ref[pl.ds((TAPS - 1 - tap) * GROUP, rows), :]


def convolve(high_ref, low_ref, w_high, w_low, rows):
    channels = w_high.shape[0] // TAPS
    total = jnp.zeros((rows, channels), F32)
    for tap in range(TAPS):
        taken = pl.ds(tap * channels, channels)
        high, low = window(high_ref, tap, rows), window(low_ref, tap, rows)
        total += dot(high, w_high[taken, :], NT)
        total += dot(low, w_high[taken, :], NT)
        total += dot(high, w_low[taken, :], NT)
    return total


def regroup(source_ref, out_ref, groups, members):
    tail = jnp.zeros((GROUP - groups, out_ref.shape[-1]), F32)
    for member in range(members):
        for lane in range(source_ref.shape[0]):
            taken = source_ref[lane, pl.ds(member, groups, stride=GROUP), :]
            out_ref[pl.ds(member * GROUP, groups), lane * LANES : (lane + 1) * LANES] = taken
        out_ref[pl.ds(member * GROUP + groups, GROUP - groups), :] = tail


def place(starts_ref, pieces, w_high, w_low):
    for index, piece in enumerate(pieces):
        high, low = split(piece[...])
        taken = pl.ds(pl.multiple_of(starts_ref[index], GROUP), piece.shape[0])
        w_high[taken, :] = high
        w_low[taken, :] = low


def conv_kernel(piece_count, masked, members, *refs):
    refs = list(refs)
    if piece_count:
        starts = refs.pop(0)
    rows_ref = refs.pop(0)
    mask_ref = refs.pop(0) if masked else None
    if piece_count:
        pieces = [refs.pop(0) for _ in range(piece_count)]
        out_ref, w_high, w_low, high, low, flat = refs
        place(starts, pieces, w_high, w_low)
    else:
        w_high, w_low, out_ref, high, low, flat = refs
    rows = rows_ref.shape[0]
    fill(rows_ref, high, low)
    total = convolve(high, low, w_high, w_low, rows)
    if masked:
        total = total * mask_ref[...].astype(F32)
    for lane in range(flat.shape[0]):
        flat[lane] = total[:, lane * LANES : (lane + 1) * LANES]
    regroup(flat, out_ref, rows // GROUP, members)


def conv(rows, mask, members, weights=None, pieces=None):
    count, channels = rows.shape
    filter_rows = TAPS * channels
    out = [jax.ShapeDtypeStruct((members * GROUP, channels), F32)]
    operands, scalars = [rows], 0
    if mask is not None:
        operands.append(mask)
    if pieces is not None:
        starts, parts = pieces
        out += [jax.ShapeDtypeStruct((filter_rows, channels), BF16)] * 2
        operands = [starts] + operands + parts
        scalars = 1
    else:
        operands += weights
    scratch = [
        pltpu.VMEM((padded_rows(count), channels), BF16),
        pltpu.VMEM((padded_rows(count), channels), BF16),
        pltpu.VMEM((channels // LANES, count, LANES), F32),
    ]
    piece_count = 0 if pieces is None else len(pieces[1])
    kernel = functools.partial(conv_kernel, piece_count, mask is not None, members)
    result = call(kernel, out, scratch, 6 * count * filter_rows * channels, *operands, scalars=scalars)
    return result if pieces is not None else result[0]


def turn_kernel(in_ref, mid_ref, *outs):
    for ref, high, low in ((in_ref, outs[0], outs[1]), (mid_ref, outs[2], outs[3])):
        for tick in range(ref.shape[0]):
            taken_high, taken_low = split(ref[tick].T)
            high[tick] = taken_high
            low[tick] = taken_low


def turned(act_in, act_mid):
    out = []
    for act in (act_in, act_mid):
        out += [jax.ShapeDtypeStruct((act.shape[0], act.shape[2], act.shape[1]), BF16)] * 2
    return call(turn_kernel, out, [], 0, act_in, act_mid)


def correlate_kernel(scale, carried, *refs):
    if carried:
        act_high, act_low, rows_ref, before, out_ref, high, low = refs
    else:
        act_high, act_low, rows_ref, out_ref, high, low = refs
    fill(rows_ref, high, low)
    rows, channels = rows_ref.shape
    for tap in range(TAPS):
        taken = pl.ds(tap * channels, channels)
        here_high, here_low = window(high, tap, rows), window(low, tap, rows)
        total = dot(act_high[...], here_high, NN)
        total += dot(act_low[...], here_high, NN)
        total += dot(act_high[...], here_low, NN)
        total *= scale
        if carried:
            total += before[taken, :]
        out_ref[taken, :] = total


def correlate(act_high, act_low, rows, scale, before=None):
    count, channels = rows.shape
    out = [jax.ShapeDtypeStruct((TAPS * channels, channels), F32)]
    scratch = [pltpu.VMEM((padded_rows(count), channels), BF16)] * 2
    operands = [act_high, act_low, rows] + ([] if before is None else [before])
    kernel = functools.partial(correlate_kernel, scale, before is not None)
    return call(kernel, out, scratch, 6 * count * TAPS * channels * channels, *operands)[0]


def by_row(values):
    spare = GROUP - values.shape[-2]
    values = jnp.pad(values, [(0, 0)] * (values.ndim - 2) + [(0, spare), (0, 0)])
    return values.reshape(values.shape[:-3] + (-1, values.shape[-1]))


def by_column(values):
    return by_row(jnp.swapaxes(values, -3, -2))


def swap(shard, bit):
    peers = lax.axis_size("dp")
    return lax.ppermute(shard, "dp", [(i, i ^ bit) for i in range(peers)])


def together(*values):
    return lax.optimization_barrier(values)


def starts_of(me, rows, pieces):
    starts = jnp.stack([(me ^ bits) * rows + offset for _, bits, offset in pieces])
    return starts.astype(jnp.int32), [piece for piece, _, _ in pieces]


def with_sibling(pieces, sibling):
    return pieces + [(piece, bits ^ 1, offset) for piece, (_, bits, offset) in zip(sibling, pieces)]


def finish(outs, ticks, height, width):
    return jnp.stack(outs).reshape(ticks, height, GROUP, -1)[:, :, :width][None, :, None]


def local_any(act_in, act_mid, relu_mask, arriving, loss_grad, w_first, w_second):
    ticks, images, height, width = act_in.shape[1:5]
    sections = lax.axis_size("section")
    is_last = lax.axis_index("section") == sections - 1
    scale = 1.0 / (ticks * images * lax.axis_size("dp"))
    start = jnp.zeros((1,), jnp.int32)
    first_pieces = (start, [lax.all_gather(w_first[0], "dp", axis=0, tiled=True)])
    second_pieces = (start, [lax.all_gather(w_second[0], "dp", axis=0, tiled=True)])
    in_high, in_low, mid_high, mid_low = turned(by_column(act_in[0, :, 0]), by_row(act_mid[0, :, 0]))
    mask = by_row(relu_mask[0, :, 0])
    loss = by_row(loss_grad[:, 0])
    incoming = by_row(arriving[0, 0])
    second = correlate(mid_high[0], mid_low[0], incoming, scale)
    pre, *w_second_parts = conv(incoming, mask[0], width, pieces=second_pieces)
    out, *w_first_parts = conv(pre, None, height, pieces=first_pieces)
    outs = [out]
    first = correlate(in_high[0], in_low[0], pre, scale)
    for tick in range(1, ticks):
        above = lax.ppermute(outs[-1], "section", [(i, i - 1) for i in range(1, sections)])
        incoming = jnp.where(is_last, loss[tick - 1], above)
        second = correlate(mid_high[tick], mid_low[tick], incoming, scale, second)
        pre = conv(incoming, mask[tick], width, weights=w_second_parts)
        first = correlate(in_high[tick], in_low[tick], pre, scale, first)
        outs.append(conv(pre, None, height, weights=w_first_parts))
    second_grad = lax.psum_scatter(second, "dp", scatter_dimension=0, tiled=True)
    first_grad = lax.psum_scatter(first, "dp", scatter_dimension=0, tiled=True)
    return finish(outs, ticks, height, width), first_grad[None], second_grad[None]


def blocks(partial, me):
    rows = partial.shape[0] // 8
    kept, sent = (
        jnp.stack([lax.dynamic_slice_in_dim(partial, (me ^ bits) * rows, rows, axis=0) for bits in group])
        for group in ((0, 2, 4, 6), (1, 3, 5, 7))
    )
    return kept, sent


def near_phase(chip):
    half = chip.shape[1] // 2
    a, b = chip[:, :half], chip[:, half:]
    return a, b, swap(jnp.stack([a[1], a[3]]), 2), swap(jnp.stack([b[2], b[3]]), 4)


def far_phase(a, b, a_there, b_there):
    a_near, a_far = a[0] + a_there[0], a[2] + a_there[1]
    b_near, b_far = b[0] + b_there[0], b[1] + b_there[1]
    return a_near, b_near, swap(a_far, 4), swap(b_far, 2)


def join(a_near, b_near, a_last, b_last):
    return jnp.concatenate([a_near + a_last, b_near + b_last], axis=0)[None]


def local_eight(act_in, act_mid, relu_mask, arriving, loss_grad, w_first, w_second):
    ticks, images, height, width = act_in.shape[1:5]
    sections = lax.axis_size("section")
    is_last = lax.axis_index("section") == sections - 1
    me = lax.axis_index("dp")
    scale = 1.0 / (ticks * images * lax.axis_size("dp"))
    one, two = w_first[0], w_second[0]
    rows = one.shape[0]
    half = rows // 2
    x_two, y_two = swap(two, 2), swap(two, 4)
    x_one, y_one = swap(one, 2), swap(one, 4)
    s_two, s_one = swap(two, 1), swap(one, 1)
    incoming = by_row(arriving[0, 0])
    mid_rows = by_row(act_mid[0, :, 0])
    in_rows = by_column(act_in[0, :, 0])
    incoming, mid_rows, in_rows, x_two, y_two = together(incoming, mid_rows, in_rows, x_two, y_two)
    ya_two, xb_two = swap(x_two[:half], 4), swap(y_two[half:], 2)
    sx_two, sy_two = swap(x_two, 1), swap(y_two, 1)
    in_high, in_low, mid_high, mid_low = turned(in_rows, mid_rows)
    second = correlate(mid_high[0], mid_low[0], incoming, scale)
    mask = by_row(relu_mask[0, :, 0])
    loss = by_row(loss_grad[:, 0])
    second, mask, loss, in_high, in_low, mid_high, mid_low, x_one, y_one = together(
        second, mask, loss, in_high, in_low, mid_high, mid_low, x_one, y_one
    )
    ya_one, xb_one = swap(x_one[:half], 4), swap(y_one[half:], 2)
    sx_one, sy_one = swap(x_one, 1), swap(y_one, 1)
    sya_two, sxb_two = swap(ya_two, 1), swap(xb_two, 1)
    own = [(two, 0, 0), (x_two, 2, 0), (y_two, 4, 0), (ya_two, 6, 0), (xb_two, 6, half)]
    pieces = with_sibling(own, [s_two, sx_two, sy_two, sya_two, sxb_two])
    pre, *w_second_parts = conv(incoming, mask[0], width, pieces=starts_of(me, rows, pieces))
    sya_one, sxb_one = swap(ya_one, 1), swap(xb_one, 1)
    own = [(one, 0, 0), (x_one, 2, 0), (y_one, 4, 0), (ya_one, 6, 0), (xb_one, 6, half)]
    pieces = with_sibling(own, [s_one, sx_one, sy_one, sya_one, sxb_one])
    out, *w_first_parts = conv(pre, None, height, pieces=starts_of(me, rows, pieces))
    outs = [out]
    first = correlate(in_high[0], in_low[0], pre, scale)
    for tick in range(1, ticks):
        above = lax.ppermute(outs[-1], "section", [(i, i - 1) for i in range(1, sections)])
        above, first = together(above, first)
        incoming = jnp.where(is_last, loss[tick - 1], above)
        second = correlate(mid_high[tick], mid_low[tick], incoming, scale, second)
        if tick < ticks - 1:
            pre = conv(incoming, mask[tick], width, weights=w_second_parts)
            first = correlate(in_high[tick], in_low[tick], pre, scale, first)
            outs.append(conv(pre, None, height, weights=w_first_parts))
    kept, sent = blocks(second, me)
    other = swap(sent, 1)
    pre = conv(incoming, mask[-1], width, weights=w_second_parts)
    first = correlate(in_high[-1], in_low[-1], pre, scale, first)
    first_kept, first_sent = blocks(first, me)
    first_other = swap(first_sent, 1)
    a, b, a_there, b_there = near_phase(kept + other)
    first_a, first_b, first_a_there, first_b_there = near_phase(first_kept + first_other)
    pre, a_there, b_there = together(pre, a_there, b_there)
    last = far_phase(a, b, a_there, b_there)
    outs.append(conv(pre, None, height, weights=w_first_parts))
    data_grad = finish(outs, ticks, height, width)
    data_grad, first_a_there, first_b_there = together(data_grad, first_a_there, first_b_there)
    first_last = far_phase(first_a, first_b, first_a_there, first_b_there)
    return data_grad, join(*first_last), join(*last)


def local(*arguments):
    return (local_eight if lax.axis_size("dp") == 8 else local_any)(*arguments)


def solution(mesh):
    return jax.shard_map(
        local,
        mesh=mesh,
        in_specs=(
            P("section", None, "dp", None, None, None),
            P("section", None, "dp", None, None, None),
            P("section", None, "dp", None, None, None),
            P("section", "dp", None, None, None),
            P(None, "dp", None, None, None),
            P("section", "dp", None),
            P("section", "dp", None),
        ),
        out_specs=(
            P("section", None, "dp", None, None, None),
            P("section", "dp", None),
            P("section", "dp", None),
        ),
        check_vma=False,
    )
```

```python
import functools

import jax
import jax.numpy as jnp
from jax import lax
from jax.experimental import pallas as pl
from jax.experimental.pallas import tpu as pltpu
from jax.sharding import PartitionSpec as P

TAPS = 7
REACH = TAPS // 2
GROUP = 16
LANES = 128
COST = 1
PREP = 60
F32 = jnp.float32
BF16 = jnp.bfloat16
NT = (((1,), (1,)), ((), ()))
NN = (((1,), (0,)), ((), ()))
VMEM = pl.BlockSpec(memory_space=pltpu.VMEM)
SMEM = pl.BlockSpec(memory_space=pltpu.SMEM)
HBM = pl.BlockSpec(memory_space=pltpu.HBM)


KNOBS = {'prep': 1, 'early2': 1, 'pretie': 1, 'fs': 1}


def knob(name, default=0):
    return KNOBS.get(name, default)


def call(kernel, out_shapes, scratch, flops, *operands, scalars=0, aliases=None, far=False, vmem=12):
    moved = sum(x.size * x.dtype.itemsize for x in operands)
    moved += sum(s.size * s.dtype.itemsize for s in out_shapes)
    return pl.pallas_call(
        kernel,
        out_shape=out_shapes,
        in_specs=[SMEM] * scalars + [HBM if far else VMEM] * (len(operands) - scalars),
        out_specs=[VMEM] * len(out_shapes),
        scratch_shapes=scratch,
        input_output_aliases=aliases or {},
        compiler_params=pltpu.CompilerParams(vmem_limit_bytes=vmem * 1024 * 1024),
        cost_estimate=pl.CostEstimate(flops=int(flops * COST), bytes_accessed=int(moved * COST), transcendentals=0),
    )(*operands)


def split(value):
    high = value.astype(BF16)
    return high, (value - high.astype(F32)).astype(BF16)


def padded_rows(rows):
    return rows + 2 * REACH * GROUP


def fill(rows_ref, high_ref, low_ref):
    rows, channels = rows_ref.shape
    edge = REACH * GROUP
    border = jnp.zeros((edge, channels), BF16)
    high, low = split(rows_ref[...])
    for ref, body in ((high_ref, high), (low_ref, low)):
        ref[pl.ds(0, edge), :] = border
        ref[pl.ds(edge, rows), :] = body
        ref[pl.ds(edge + rows, edge), :] = border


def dot(a, b, dims):
    return lax.dot_general(a, b, dims, preferred_element_type=F32)


def window(ref, tap, rows):
    return ref[pl.ds((TAPS - 1 - tap) * GROUP, rows), :]


def convolve(high_ref, low_ref, w_high, w_low, rows, columns):
    channels = w_high.shape[0] // TAPS
    width = columns[1] - columns[0]
    total = jnp.zeros((rows, width), F32)
    for tap in range(TAPS):
        taken = pl.ds(tap * channels + columns[0], width)
        high, low = window(high_ref, tap, rows), window(low_ref, tap, rows)
        total += dot(high, w_high[taken, :], NT)
        total += dot(low, w_high[taken, :], NT)
        total += dot(high, w_low[taken, :], NT)
    return total


def regroup(source_ref, out_ref, groups, members):
    tail = jnp.zeros((GROUP - groups, out_ref.shape[-1]), F32)
    for member in range(members):
        for lane in range(source_ref.shape[0]):
            taken = source_ref[lane, pl.ds(member, groups, stride=GROUP), :]
            out_ref[pl.ds(member * GROUP, groups), lane * LANES : (lane + 1) * LANES] = taken
        out_ref[pl.ds(member * GROUP + groups, GROUP - groups), :] = tail


def place(starts_ref, granule, pieces, w_high, w_low):
    index = 0
    for piece in pieces:
        for begin in range(0, piece.shape[0], granule):
            high, low = split(piece[pl.ds(begin, granule), :])
            taken = pl.ds(pl.multiple_of(starts_ref[index], GROUP), granule)
            w_high[taken, :] = high
            w_low[taken, :] = low
            index += 1


def place_kernel(granule, starts_ref, *refs):
    place(starts_ref, granule, refs[:-2], *refs[-2:])


def placed(granule, starts, pieces, filter_rows):
    out = [jax.ShapeDtypeStruct((filter_rows, pieces[0].shape[1]), BF16)] * 2
    return call(functools.partial(place_kernel, granule), out, [], 0, starts, *pieces, scalars=1)


def conv_kernel(piece_count, granule, carried, masked, members, columns, *refs):
    refs = list(refs)
    starts = refs.pop(0) if piece_count else None
    rows_ref = refs.pop(0)
    mask_ref = refs.pop(0) if masked else None
    pieces = [refs.pop(0) for _ in range(piece_count)]
    if carried:
        w_high, w_low = refs.pop(0), refs.pop(0)
    out_ref = refs.pop(0)
    if piece_count:
        w_high, w_low = refs.pop(0), refs.pop(0)
        place(starts, granule, pieces, w_high, w_low)
    high, low, flat = refs
    rows = rows_ref.shape[0]
    fill(rows_ref, high, low)
    total = convolve(high, low, w_high, w_low, rows, columns)
    if masked:
        total = total * mask_ref[...].astype(F32)
    for lane in range(flat.shape[0]):
        flat[lane] = total[:, lane * LANES : (lane + 1) * LANES]
    regroup(flat, out_ref, rows // GROUP, members)


def conv(rows, mask, members, weights=None, pieces=None, columns=None):
    count, channels = rows.shape
    filter_rows = TAPS * channels
    columns = columns or (0, channels)
    width = columns[1] - columns[0]
    granule, starts, parts = pieces or (0, None, [])
    operands = [rows] + ([] if mask is None else [mask]) + parts + list(weights or [])
    out = [jax.ShapeDtypeStruct((members * GROUP, width), F32)]
    aliases = {}
    if parts:
        operands = [starts] + operands
        out += [jax.ShapeDtypeStruct((filter_rows, channels), BF16)] * 2
        if weights:
            aliases = {len(operands) - 2: 1, len(operands) - 1: 2}
    scratch = [
        pltpu.VMEM((padded_rows(count), channels), BF16),
        pltpu.VMEM((padded_rows(count), channels), BF16),
        pltpu.VMEM((width // LANES, count, LANES), F32),
    ]
    kernel = functools.partial(
        conv_kernel, len(parts), granule, bool(weights), mask is not None, members, columns
    )
    flops = 6 * count * filter_rows * width
    result = call(kernel, out, scratch, flops, *operands, scalars=1 if parts else 0, aliases=aliases)
    return result if parts else result[0]


def spread(line_ref, start, height, width, out_ref):
    out_ref[...] = jnp.zeros_like(out_ref)
    for row in range(height):
        out_ref[pl.ds(row * GROUP, width), :] = line_ref[pl.ds(start + row * width, width), 0, :]


def prepare_kernel(height, width, *refs):
    sources, refs = refs[:5], refs[5:]
    row_outs, turned_outs, refs = refs[:3], refs[3:7], refs[7:]
    lines, (flat, grouped, scratch, arrived) = refs[:5], refs[5:]
    copies = [pltpu.make_async_copy(source, held, arrived.at[index]) for index, (source, held) in enumerate(zip(sources, lines))]
    for copy in copies:
        copy.start()
    for copy, held, out in zip(copies, lines, row_outs):
        copy.wait()
        for index in range(out.shape[0]):
            spread(held, index * height * width, height, width, out.at[index])
    in_line, mid_line = lines[3:]
    copies[3].wait()
    copies[4].wait()
    for tick in range(turned_outs[0].shape[0]):
        start = tick * height * width
        spread(in_line, start, height, width, scratch)
        for lane in range(flat.shape[0]):
            flat[lane] = scratch[:, lane * LANES : (lane + 1) * LANES]
        regroup(flat, grouped, height, width)
        turned_outs[0][tick], turned_outs[1][tick] = split(grouped[...].T)
        spread(mid_line, start, height, width, scratch)
        turned_outs[2][tick], turned_outs[3][tick] = split(scratch[...].T)


def prepare(height, width, mask, loss, came, act_in, act_mid):
    sources = [came, mask, loss, act_in, act_mid]
    ticks, channels = act_in.shape[0] // (height * width), act_in.shape[2]
    out = [jax.ShapeDtypeStruct((x.shape[0] // (height * width), height * GROUP, channels), x.dtype) for x in sources[:3]]
    out += [jax.ShapeDtypeStruct((ticks, channels, width * GROUP), BF16)] * 2
    out += [jax.ShapeDtypeStruct((ticks, channels, height * GROUP), BF16)] * 2
    scratch = [pltpu.VMEM(x.shape, x.dtype) for x in sources]
    scratch += [
        pltpu.VMEM((channels // LANES, height * GROUP, LANES), F32),
        pltpu.VMEM((width * GROUP, channels), F32),
        pltpu.VMEM((height * GROUP, channels), F32),
        pltpu.SemaphoreType.DMA((len(sources),)),
    ]
    kernel = functools.partial(prepare_kernel, height, width)
    came, mask, loss, *parts = call(kernel, out, scratch, 0, *sources, far=True, vmem=PREP)
    return mask, loss, came[0], *parts


def last_kernel(height, width, *refs):
    rows_ref, w_high, w_low = refs[:3]
    before, (line_ref, high, low, flat) = refs[3:-4], refs[-4:]
    for tick, ref in enumerate(before):
        for row in range(height):
            start = (tick * height + row) * width
            line_ref[pl.ds(start, width), 0, :] = ref[pl.ds(row * GROUP, width), :]
    rows = rows_ref.shape[0]
    fill(rows_ref, high, low)
    total = convolve(high, low, w_high, w_low, rows, (0, rows_ref.shape[1]))
    lanes = flat.shape[0]
    for lane in range(lanes):
        flat[lane] = total[:, lane * LANES : (lane + 1) * LANES]
    for row in range(height):
        start = (len(before) * height + row) * width
        taken = [flat[lane, pl.ds(row, width, stride=GROUP), :] for lane in range(lanes)]
        line_ref[pl.ds(start, width), 0, :] = jnp.concatenate(taken, axis=1)


def last_conv(rows, weights, before, height, width):
    count, channels = rows.shape
    out = [jax.ShapeDtypeStruct(((len(before) + 1) * height * width, 1, channels), F32)]
    scratch = [
        pltpu.VMEM((padded_rows(count), channels), BF16),
        pltpu.VMEM((padded_rows(count), channels), BF16),
        pltpu.VMEM((channels // LANES, count, LANES), F32),
    ]
    flops = 6 * count * TAPS * channels * channels
    kernel = functools.partial(last_kernel, height, width)
    return call(kernel, out, scratch, flops, rows, *weights, *before)[0]


def correlate_kernel(scale, carried, dealt, *refs):
    refs = list(refs)
    starts = refs.pop(0) if dealt else None
    act_high, act_low, rows_ref = refs[:3]
    before = refs[3] if carried else None
    out_ref, high, low = refs[3 + carried :]
    fill(rows_ref, high, low)
    rows, channels = rows_ref.shape
    for tap in range(TAPS):
        taken = pl.ds(tap * channels, channels)
        here_high, here_low = window(high, tap, rows), window(low, tap, rows)
        total = dot(act_high[...], here_high, NN)
        total += dot(act_low[...], here_high, NN)
        total += dot(act_high[...], here_low, NN)
        total *= scale
        if carried:
            total += before[taken, :]
        if not dealt:
            out_ref[taken, :] = total
            continue
        block_rows = out_ref.shape[2]
        begin, end = tap * channels, (tap + 1) * channels
        for block in range(begin // block_rows, -(-end // block_rows)):
            first, last = max(begin, block * block_rows), min(end, (block + 1) * block_rows)
            into = pl.ds(first - block * block_rows, last - first)
            distance = jnp.bitwise_xor(block, starts[0])
            place_at = (jnp.bitwise_and(distance, 1), jnp.right_shift(distance, 1), into)
            out_ref[place_at] = total[first - begin : last - begin, :]


def correlate(act_high, act_low, rows, scale, before=None, starts=None):
    count, channels = rows.shape
    filter_rows = TAPS * channels
    scratch = [pltpu.VMEM((padded_rows(count), channels), BF16)] * 2
    operands = [act_high, act_low, rows] + ([] if before is None else [before])
    if starts is None:
        out = [jax.ShapeDtypeStruct((filter_rows, channels), F32)]
    else:
        out = [jax.ShapeDtypeStruct((2, 4, filter_rows // 8, channels), F32)]
        operands = [starts] + operands
    kernel = functools.partial(correlate_kernel, scale, before is not None, starts is not None)
    flops = 6 * count * filter_rows * channels
    result = call(kernel, out, scratch, flops, *operands, scalars=0 if starts is None else 1)
    return result[0]


def both_kernel(scale, *refs):
    two, one, (second_ref, first_ref, high, low) = refs[:3], refs[3:6], refs[6:]
    correlate_kernel(scale, False, False, *two, second_ref, high, low)
    correlate_kernel(scale, False, False, *one, first_ref, high, low)


def correlate_both(mid_parts, incoming, in_parts, pre, scale):
    count, channels = incoming.shape
    out = [jax.ShapeDtypeStruct((TAPS * channels, channels), F32)] * 2
    scratch = [pltpu.VMEM((padded_rows(count), channels), BF16)] * 2
    operands = [*mid_parts, incoming, *in_parts, pre]
    flops = 12 * count * TAPS * channels * channels
    return call(functools.partial(both_kernel, scale), out, scratch, flops, *operands)


def line(values):
    return values.reshape(-1, 1, values.shape[-1])


def swap(shard, bit):
    peers = lax.axis_size("dp")
    return lax.ppermute(shard, "dp", [(i, i ^ bit) for i in range(peers)])


def together(*values):
    return lax.optimization_barrier(values)


def starts_of(me, rows, granule, pieces):
    starts = []
    for piece, bits, offset in pieces:
        bits = bits if isinstance(bits, tuple) else (bits,)
        for begin in range(0, piece.shape[0], granule):
            block = me ^ bits[begin // rows]
            starts.append(block * rows + offset + begin % rows)
    return granule, jnp.stack(starts).astype(jnp.int32), [piece for piece, _, _ in pieces]


def local_any(act_in, act_mid, relu_mask, arriving, loss_grad, w_first, w_second):
    ticks, images, height, width = act_in.shape[1:5]
    sections = lax.axis_size("section")
    is_last = lax.axis_index("section") == sections - 1
    scale = 1.0 / (ticks * images * lax.axis_size("dp"))
    start = jnp.zeros((1,), jnp.int32)
    filter_rows = w_first.shape[1] * lax.axis_size("dp")
    first_pieces = (filter_rows, start, [lax.all_gather(w_first[0], "dp", axis=0, tiled=True)])
    second_pieces = (filter_rows, start, [lax.all_gather(w_second[0], "dp", axis=0, tiled=True)])
    mask, loss, incoming, in_high, in_low, mid_high, mid_low = prepare(
        height, width, line(relu_mask), line(loss_grad), line(arriving), line(act_in), line(act_mid)
    )
    second = correlate(mid_high[0], mid_low[0], incoming, scale)
    pre, *second_parts = conv(incoming, mask[0], width, pieces=second_pieces)
    out, *first_parts = conv(pre, None, height, pieces=first_pieces)
    outs = [out]
    first = correlate(in_high[0], in_low[0], pre, scale)
    for tick in range(1, ticks):
        above = lax.ppermute(outs[-1], "section", [(i, i - 1) for i in range(1, sections)])
        incoming = jnp.where(is_last, loss[tick - 1], above)
        second = correlate(mid_high[tick], mid_low[tick], incoming, scale, second)
        pre = conv(incoming, mask[tick], width, weights=second_parts)
        first = correlate(in_high[tick], in_low[tick], pre, scale, first)
        if tick < ticks - 1:
            outs.append(conv(pre, None, height, weights=first_parts))
    data_grad = last_conv(pre, first_parts, outs, height, width).reshape(act_in.shape)
    second_grad = lax.psum_scatter(second, "dp", scatter_dimension=0, tiled=True)
    first_grad = lax.psum_scatter(first, "dp", scatter_dimension=0, tiled=True)
    return data_grad, first_grad[None], second_grad[None]


def near_phase(chip):
    half = chip.shape[1] // 2
    a, b = chip[:, :half], chip[:, half:]
    return a, b, swap(jnp.stack([a[1], a[3]]), 2), swap(jnp.stack([b[2], b[3]]), 4)


def far_phase(a, b, a_there, b_there):
    a_near, a_far = a[0] + a_there[0], a[2] + a_there[1]
    if knob("fs"):
        a_far, b_there = together(a_far, b_there)
    b_near, b_far = b[0] + b_there[0], b[1] + b_there[1]
    return a_near, b_near, swap(a_far, 4), swap(b_far, 2)


def join(a_near, b_near, a_last, b_last):
    return jnp.concatenate([a_near + a_last, b_near + b_last], axis=0)[None]


def far_pieces(x_piece, y_piece):
    half = x_piece.shape[0] // 2
    return swap(x_piece[:half], 4), swap(y_piece[half:], 2)


def local_eight(act_in, act_mid, relu_mask, arriving, loss_grad, w_first, w_second):
    ticks, images, height, width = act_in.shape[1:5]
    channels = act_in.shape[-1]
    filter_rows = TAPS * channels
    sections = lax.axis_size("section")
    is_last = lax.axis_index("section") == sections - 1
    me = lax.axis_index("dp")
    scale = 1.0 / (ticks * images * lax.axis_size("dp"))
    one, two = w_first[0], w_second[0]
    rows = one.shape[0]
    half = rows // 2
    owners = jnp.reshape(me, (1,)).astype(jnp.int32)
    x_two, y_two = swap(two, 2), swap(two, 4)
    x_one, y_one = swap(one, 2), swap(one, 4)
    s_two, s_one = swap(two, 1), swap(one, 1)
    mask, loss, incoming, in_high, in_low, mid_high, mid_low = prepare(
        height, width, line(relu_mask), line(loss_grad), line(arriving), line(act_in), line(act_mid)
    )
    if knob("mask"):
        mask = [mask[tick] for tick in range(ticks)]
        if knob("mask") == 2:
            *mask, y_two = together(*mask, y_two)
    if knob("prep") == 4:
        mask, loss, incoming, x_two, in_high, in_low, mid_high, mid_low = together(
            mask, loss, incoming, x_two, in_high, in_low, mid_high, mid_low
        )
    elif knob("prep") == 0:
        mask, loss, incoming, x_two, y_two = together(mask, loss, incoming, x_two, y_two)
    elif knob("prep") == 1:
        mask, loss, incoming, x_two, y_two, in_high, in_low, mid_high, mid_low = together(
            mask, loss, incoming, x_two, y_two, in_high, in_low, mid_high, mid_low
        )
    elif knob("prep") == 2:
        mask, loss, incoming, x_two, y_two, s_two, in_high, in_low, mid_high, mid_low = together(
            mask, loss, incoming, x_two, y_two, s_two, in_high, in_low, mid_high, mid_low
        )
    elif knob("prep") == 3:
        mask, loss, incoming, x_two, y_two, s_two = together(mask, loss, incoming, x_two, y_two, s_two)
    ya_two, xb_two = far_pieces(x_two, y_two)
    if knob("near") == 0:
        sx_two, sy_two = swap(x_two, 1), swap(y_two, 1)
        near_two = [(x_two, 2, 0), (y_two, 4, 0), (sx_two, 3, 0), (sy_two, 5, 0)]
    else:
        n_two = jnp.concatenate([x_two, y_two])
        near_two = [(n_two, (2, 4), 0), (swap(n_two, 1), (3, 5), 0)]
    come = [(two, 0, 0), (s_two, 1, 0)] + near_two
    second_parts = None
    if knob("early2"):
        second_parts = placed(*starts_of(me, rows, rows, come), filter_rows)
        come = []
    if knob("g2") == 0:
        second = correlate(mid_high[0], mid_low[0], incoming, scale)
    if knob("tie2") == 1:
        x_one, y_one, second = together(x_one, y_one, second)
    elif knob("tie2") == 2:
        x_one, y_one, *second_parts = together(x_one, y_one, *second_parts)
    elif knob("tie2") == 3:
        x_one, y_one, in_high, in_low, mid_high, mid_low = together(
            x_one, y_one, in_high, in_low, mid_high, mid_low
        )
    if knob("late1") == 1:
        s_one = swap(together(one, x_two)[0], 1)
    elif knob("late1") == 2:
        s_one = swap(together(one, x_one, y_one)[0], 1)
    if knob("far1") == 0:
        ya_one, xb_one = far_pieces(x_one, y_one)
        far_one = [(ya_one, 6, 0), (xb_one, 6, half)]
    else:
        d_one = swap(together(one, x_two, y_two)[0], 6)
        far_one = [(d_one, 6, 0)]
    if knob("near") == 0:
        sx_one, sy_one = swap(x_one, 1), swap(y_one, 1)
        near_one = [(x_one, 2, 0), (y_one, 4, 0), (sx_one, 3, 0), (sy_one, 5, 0)]
    else:
        n_one = jnp.concatenate([x_one, y_one])
        near_one = [(n_one, (2, 4), 0), (swap(n_one, 1), (3, 5), 0)]
    if knob("farcat"):
        f_two = jnp.concatenate([ya_two, xb_two])
        come += [(f_two, 6, 0), (swap(f_two, 1), 7, 0)]
    else:
        sya_two, sxb_two = swap(ya_two, 1), swap(xb_two, 1)
        come += [(ya_two, 6, 0), (xb_two, 6, half), (sya_two, 7, 0), (sxb_two, 7, half)]
    pre, *second_parts = conv(incoming, mask[0], width, weights=second_parts, pieces=starts_of(me, rows, half, come))
    come = [(one, 0, 0), (s_one, 1, 0)] + near_one
    first_parts = None
    if knob("early1"):
        first_parts = placed(*starts_of(me, rows, rows, come), filter_rows)
        come = []
    if knob("pretie") == 1:
        ends, pre = [piece for piece, _, _ in far_one], pre
        *ends, pre = together(*ends, pre)
        far_one = [(end, bits, offset) for end, (_, bits, offset) in zip(ends, far_one)]
    elif knob("pretie") == 2:
        *ends, pre, first_high, first_low = together(*[piece for piece, _, _ in far_one], pre, *first_parts)
        first_parts = [first_high, first_low]
        far_one = [(end, bits, offset) for end, (_, bits, offset) in zip(ends, far_one)]
    if knob("farcat") and len(far_one) == 2:
        far_one = [(jnp.concatenate([piece for piece, _, _ in far_one]), 6, 0)]
    come += far_one + [(swap(piece, 1), bits ^ 1, offset) for piece, bits, offset in far_one]
    out, *first_parts = conv(pre, None, height, weights=first_parts, pieces=starts_of(me, rows, half, come))
    outs = [out]
    in_high, in_low, pre, _ = together(in_high, in_low, pre, out)
    if knob("g2") == 1:
        mid_high, mid_low, _ = together(mid_high, mid_low, out)
        second = correlate(mid_high[0], mid_low[0], incoming, scale)
    if knob("g2") == 2:
        mid_high, mid_low, _ = together(mid_high, mid_low, out)
        second, first = correlate_both((mid_high[0], mid_low[0]), incoming, (in_high[0], in_low[0]), pre, scale)
    else:
        first = correlate(in_high[0], in_low[0], pre, scale)
    for tick in range(1, ticks):
        above = lax.ppermute(outs[-1], "section", [(i, i - 1) for i in range(1, sections)])
        above, first, second = together(above, first, second)
        incoming = jnp.where(is_last, loss[tick - 1], above)
        if tick < ticks - 1:
            second = correlate(mid_high[tick], mid_low[tick], incoming, scale, second)
            pre = conv(incoming, mask[tick], width, weights=second_parts)
            first = correlate(in_high[tick], in_low[tick], pre, scale, first)
            outs.append(conv(pre, None, height, weights=first_parts))
    dealt = correlate(mid_high[-1], mid_low[-1], incoming, scale, second, owners)
    kept, other = dealt[0], swap(dealt[1], 1)
    pre = conv(incoming, mask[-1], width, weights=second_parts)
    first_dealt = correlate(in_high[-1], in_low[-1], pre, scale, first, owners)
    first_kept, first_other = first_dealt[0], swap(first_dealt[1], 1)
    a, b, a_there, b_there = near_phase(kept + other)
    if knob("rs") == 3:
        data_grad = last_conv(pre, first_parts, outs, height, width)
        first_other, data_grad = together(first_other, data_grad)
    first_a, first_b, first_a_there, first_b_there = near_phase(first_kept + first_other)
    if knob("rs") == 0:
        pre, a_there, b_there = together(pre, a_there, b_there)
    elif knob("rs") == 1:
        pre, first_a_there, first_b_there = together(pre, first_a_there, first_b_there)
    elif knob("rs") == 2:
        pre, first_other = together(pre, first_other)
    last = far_phase(a, b, a_there, b_there)
    if knob("rs") != 3:
        data_grad = last_conv(pre, first_parts, outs, height, width)
    if knob("rs") == 2:
        data_grad, first_a_there, first_b_there = together(data_grad, first_a_there, first_b_there)
    first_last = far_phase(first_a, first_b, first_a_there, first_b_there)
    if knob("join"):
        both = together(*last, *first_last)
        last, first_last = both[:4], both[4:]
    return data_grad.reshape((1, ticks, images, height, width, channels)), join(*first_last), join(*last)


def local(*arguments):
    return (local_eight if lax.axis_size("dp") == 8 else local_any)(*arguments)


def solution(mesh):
    return jax.shard_map(
        local,
        mesh=mesh,
        in_specs=(
            P("section", None, "dp", None, None, None),
            P("section", None, "dp", None, None, None),
            P("section", None, "dp", None, None, None),
            P("section", "dp", None, None, None),
            P(None, "dp", None, None, None),
            P("section", "dp", None),
            P("section", "dp", None),
        ),
        out_specs=(
            P("section", None, "dp", None, None, None),
            P("section", "dp", None),
            P("section", "dp", None),
        ),
        check_vma=False,
    )
```

```python
import functools

import jax
import jax.numpy as jnp
from jax import lax
from jax.experimental import pallas as pl
from jax.experimental.pallas import tpu as pltpu
from jax.sharding import PartitionSpec as P

TAPS = 7
REACH = TAPS // 2
GROUP = 16
LANES = 128
F32 = jnp.float32
BF16 = jnp.bfloat16
NT = (((1,), (1,)), ((), ()))
NN = (((1,), (0,)), ((), ()))
VMEM = pl.BlockSpec(memory_space=pltpu.VMEM)
SMEM = pl.BlockSpec(memory_space=pltpu.SMEM)
HBM = pl.BlockSpec(memory_space=pltpu.HBM)


def call(kernel, out_shapes, scratch, flops, *operands, scalars=0, aliases=None, far=False, vmem=12):
    moved = sum(x.size * x.dtype.itemsize for x in operands)
    moved += sum(s.size * s.dtype.itemsize for s in out_shapes)
    return pl.pallas_call(
        kernel,
        out_shape=out_shapes,
        in_specs=[SMEM] * scalars + [HBM if far else VMEM] * (len(operands) - scalars),
        out_specs=[VMEM] * len(out_shapes),
        scratch_shapes=scratch,
        input_output_aliases=aliases or {},
        compiler_params=pltpu.CompilerParams(vmem_limit_bytes=vmem * 1024 * 1024),
        cost_estimate=pl.CostEstimate(flops=flops, bytes_accessed=moved, transcendentals=0),
    )(*operands)


def split(value):
    high = value.astype(BF16)
    return high, (value - high.astype(F32)).astype(BF16)


def padded_rows(rows):
    return rows + 2 * REACH * GROUP


def fill(rows_ref, high_ref, low_ref):
    rows, channels = rows_ref.shape
    edge = REACH * GROUP
    border = jnp.zeros((edge, channels), BF16)
    high, low = split(rows_ref[...])
    for ref, body in ((high_ref, high), (low_ref, low)):
        ref[pl.ds(0, edge), :] = border
        ref[pl.ds(edge, rows), :] = body
        ref[pl.ds(edge + rows, edge), :] = border


def dot(a, b, dims):
    return lax.dot_general(a, b, dims, preferred_element_type=F32)


def window(ref, tap, rows):
    return ref[pl.ds((TAPS - 1 - tap) * GROUP, rows), :]


def convolve(high_ref, low_ref, w_high, w_low, rows, columns):
    channels = w_high.shape[0] // TAPS
    width = columns[1] - columns[0]
    total = jnp.zeros((rows, width), F32)
    for tap in range(TAPS):
        taken = pl.ds(tap * channels + columns[0], width)
        high, low = window(high_ref, tap, rows), window(low_ref, tap, rows)
        total += dot(high, w_high[taken, :], NT)
        total += dot(low, w_high[taken, :], NT)
        total += dot(high, w_low[taken, :], NT)
    return total


def regroup(source_ref, out_ref, groups, members):
    tail = jnp.zeros((GROUP - groups, out_ref.shape[-1]), F32)
    for member in range(members):
        for lane in range(source_ref.shape[0]):
            taken = source_ref[lane, pl.ds(member, groups, stride=GROUP), :]
            out_ref[pl.ds(member * GROUP, groups), lane * LANES : (lane + 1) * LANES] = taken
        out_ref[pl.ds(member * GROUP + groups, GROUP - groups), :] = tail


def place(starts_ref, granule, pieces, w_high, w_low):
    index = 0
    for piece in pieces:
        for begin in range(0, piece.shape[0], granule):
            high, low = split(piece[pl.ds(begin, granule), :])
            taken = pl.ds(pl.multiple_of(starts_ref[index], GROUP), granule)
            w_high[taken, :] = high
            w_low[taken, :] = low
            index += 1


def place_kernel(granule, starts_ref, *refs):
    place(starts_ref, granule, refs[:-2], *refs[-2:])


def placed(granule, starts, pieces, filter_rows):
    out = [jax.ShapeDtypeStruct((filter_rows, pieces[0].shape[1]), BF16)] * 2
    return call(functools.partial(place_kernel, granule), out, [], 0, starts, *pieces, scalars=1)


def conv_kernel(piece_count, granule, carried, masked, members, columns, *refs):
    refs = list(refs)
    starts = refs.pop(0) if piece_count else None
    rows_ref = refs.pop(0)
    mask_ref = refs.pop(0) if masked else None
    pieces = [refs.pop(0) for _ in range(piece_count)]
    if carried:
        w_high, w_low = refs.pop(0), refs.pop(0)
    out_ref = refs.pop(0)
    if piece_count:
        w_high, w_low = refs.pop(0), refs.pop(0)
        place(starts, granule, pieces, w_high, w_low)
    high, low, flat = refs
    rows = rows_ref.shape[0]
    fill(rows_ref, high, low)
    total = convolve(high, low, w_high, w_low, rows, columns)
    if masked:
        total = total * mask_ref[...].astype(F32)
    for lane in range(flat.shape[0]):
        flat[lane] = total[:, lane * LANES : (lane + 1) * LANES]
    regroup(flat, out_ref, rows // GROUP, members)


def conv(rows, mask, members, weights=None, pieces=None, columns=None):
    count, channels = rows.shape
    filter_rows = TAPS * channels
    columns = columns or (0, channels)
    width = columns[1] - columns[0]
    granule, starts, parts = pieces or (0, None, [])
    operands = [rows] + ([] if mask is None else [mask]) + parts + list(weights or [])
    out = [jax.ShapeDtypeStruct((members * GROUP, width), F32)]
    aliases = {}
    if parts:
        operands = [starts] + operands
        out += [jax.ShapeDtypeStruct((filter_rows, channels), BF16)] * 2
        if weights:
            aliases = {len(operands) - 2: 1, len(operands) - 1: 2}
    scratch = [
        pltpu.VMEM((padded_rows(count), channels), BF16),
        pltpu.VMEM((padded_rows(count), channels), BF16),
        pltpu.VMEM((width // LANES, count, LANES), F32),
    ]
    kernel = functools.partial(
        conv_kernel, len(parts), granule, bool(weights), mask is not None, members, columns
    )
    flops = 6 * count * filter_rows * width
    result = call(kernel, out, scratch, flops, *operands, scalars=1 if parts else 0, aliases=aliases)
    return result if parts else result[0]


def spread(line_ref, start, height, width, out_ref):
    tail = jnp.zeros((GROUP - width, out_ref.shape[-1]), line_ref.dtype)
    for row in range(height):
        taken = jnp.concatenate([line_ref[pl.ds(start + row * width, width), 0, :], tail])
        out_ref[pl.ds(row * GROUP, GROUP), :] = taken.astype(out_ref.dtype)


def prepare_kernel(height, width, *refs):
    sources, refs = refs[:5], refs[5:]
    row_outs, turned_outs, refs = refs[:3], refs[3:7], refs[7:]
    lines, (flat, grouped, scratch, arrived) = refs[:5], refs[5:]
    copies = [pltpu.make_async_copy(source, held, arrived.at[index]) for index, (source, held) in enumerate(zip(sources, lines))]
    for copy in copies:
        copy.start()
    for copy, held, out in zip(copies, lines, row_outs):
        copy.wait()
        for index in range(out.shape[0]):
            spread(held, index * height * width, height, width, out.at[index])
    in_line, mid_line = lines[3:]
    copies[3].wait()
    copies[4].wait()
    for tick in range(turned_outs[0].shape[0]):
        start = tick * height * width
        spread(in_line, start, height, width, scratch)
        for lane in range(flat.shape[0]):
            flat[lane] = scratch[:, lane * LANES : (lane + 1) * LANES]
        regroup(flat, grouped, height, width)
        turned_outs[0][tick], turned_outs[1][tick] = split(grouped[...].T)
        spread(mid_line, start, height, width, scratch)
        turned_outs[2][tick], turned_outs[3][tick] = split(scratch[...].T)


def prepare(height, width, mask, loss, came, act_in, act_mid):
    sources = [came, mask, loss, act_in, act_mid]
    ticks, channels = act_in.shape[0] // (height * width), act_in.shape[2]
    out = [jax.ShapeDtypeStruct((x.shape[0] // (height * width), height * GROUP, channels), x.dtype) for x in sources[:3]]
    out[1] = jax.ShapeDtypeStruct(out[1].shape, BF16)
    out += [jax.ShapeDtypeStruct((ticks, channels, width * GROUP), BF16)] * 2
    out += [jax.ShapeDtypeStruct((ticks, channels, height * GROUP), BF16)] * 2
    scratch = [pltpu.VMEM(x.shape, x.dtype) for x in sources]
    scratch += [
        pltpu.VMEM((channels // LANES, height * GROUP, LANES), F32),
        pltpu.VMEM((width * GROUP, channels), F32),
        pltpu.VMEM((height * GROUP, channels), F32),
        pltpu.SemaphoreType.DMA((len(sources),)),
    ]
    kernel = functools.partial(prepare_kernel, height, width)
    came, mask, loss, *parts = call(kernel, out, scratch, 0, *sources, far=True, vmem=60)
    return mask, loss, came[0], *parts


def last_kernel(height, width, *refs):
    rows_ref, w_high, w_low = refs[:3]
    before, (line_ref, high, low, flat) = refs[3:-4], refs[-4:]
    for tick, ref in enumerate(before):
        for row in range(height):
            start = (tick * height + row) * width
            line_ref[pl.ds(start, width), 0, :] = ref[pl.ds(row * GROUP, width), :]
    rows = rows_ref.shape[0]
    fill(rows_ref, high, low)
    total = convolve(high, low, w_high, w_low, rows, (0, rows_ref.shape[1]))
    lanes = flat.shape[0]
    for lane in range(lanes):
        flat[lane] = total[:, lane * LANES : (lane + 1) * LANES]
    for row in range(height):
        start = (len(before) * height + row) * width
        taken = [flat[lane, pl.ds(row, width, stride=GROUP), :] for lane in range(lanes)]
        line_ref[pl.ds(start, width), 0, :] = jnp.concatenate(taken, axis=1)


def last_conv(rows, weights, before, height, width):
    count, channels = rows.shape
    out = [jax.ShapeDtypeStruct(((len(before) + 1) * height * width, 1, channels), F32)]
    scratch = [
        pltpu.VMEM((padded_rows(count), channels), BF16),
        pltpu.VMEM((padded_rows(count), channels), BF16),
        pltpu.VMEM((channels // LANES, count, LANES), F32),
    ]
    flops = 6 * count * TAPS * channels * channels
    kernel = functools.partial(last_kernel, height, width)
    return call(kernel, out, scratch, flops, rows, *weights, *before)[0]


def correlate_kernel(scale, carried, dealt, *refs):
    refs = list(refs)
    starts = refs.pop(0) if dealt else None
    act_high, act_low, rows_ref = refs[:3]
    before = refs[3] if carried else None
    out_ref, high, low = refs[3 + carried :]
    fill(rows_ref, high, low)
    rows, channels = rows_ref.shape
    for tap in range(TAPS):
        taken = pl.ds(tap * channels, channels)
        here_high, here_low = window(high, tap, rows), window(low, tap, rows)
        total = dot(act_high[...], here_high, NN)
        total += dot(act_low[...], here_high, NN)
        total += dot(act_high[...], here_low, NN)
        total *= scale
        if carried:
            total += before[taken, :]
        if not dealt:
            out_ref[taken, :] = total
            continue
        block_rows = out_ref.shape[2]
        begin, end = tap * channels, (tap + 1) * channels
        for block in range(begin // block_rows, -(-end // block_rows)):
            first, last = max(begin, block * block_rows), min(end, (block + 1) * block_rows)
            into = pl.ds(first - block * block_rows, last - first)
            distance = jnp.bitwise_xor(block, starts[0])
            place_at = (jnp.bitwise_and(distance, 1), jnp.right_shift(distance, 1), into)
            out_ref[place_at] = total[first - begin : last - begin, :]


def correlate(act_high, act_low, rows, scale, before=None, starts=None):
    count, channels = rows.shape
    filter_rows = TAPS * channels
    scratch = [pltpu.VMEM((padded_rows(count), channels), BF16)] * 2
    operands = [act_high, act_low, rows] + ([] if before is None else [before])
    if starts is None:
        out = [jax.ShapeDtypeStruct((filter_rows, channels), F32)]
    else:
        out = [jax.ShapeDtypeStruct((2, 4, filter_rows // 8, channels), F32)]
        operands = [starts] + operands
    kernel = functools.partial(correlate_kernel, scale, before is not None, starts is not None)
    flops = 6 * count * filter_rows * channels
    result = call(kernel, out, scratch, flops, *operands, scalars=0 if starts is None else 1)
    return result[0]


def both_kernel(scale, *refs):
    two, one, (second_ref, first_ref, high, low) = refs[:3], refs[3:6], refs[6:]
    correlate_kernel(scale, False, False, *two, second_ref, high, low)
    correlate_kernel(scale, False, False, *one, first_ref, high, low)


def correlate_both(mid_parts, incoming, in_parts, pre, scale):
    count, channels = incoming.shape
    out = [jax.ShapeDtypeStruct((TAPS * channels, channels), F32)] * 2
    scratch = [pltpu.VMEM((padded_rows(count), channels), BF16)] * 2
    operands = [*mid_parts, incoming, *in_parts, pre]
    flops = 12 * count * TAPS * channels * channels
    return call(functools.partial(both_kernel, scale), out, scratch, flops, *operands)


def line(values):
    return values.reshape(-1, 1, values.shape[-1])


def swap(shard, bit):
    peers = lax.axis_size("dp")
    return lax.ppermute(shard, "dp", [(i, i ^ bit) for i in range(peers)])


def together(*values):
    return lax.optimization_barrier(values)


def starts_of(me, rows, granule, pieces):
    starts = []
    for piece, bits, offset in pieces:
        bits = bits if isinstance(bits, tuple) else (bits,)
        for begin in range(0, piece.shape[0], granule):
            block = me ^ bits[begin // rows]
            starts.append(block * rows + offset + begin % rows)
    return granule, jnp.stack(starts).astype(jnp.int32), [piece for piece, _, _ in pieces]


def local_any(act_in, act_mid, relu_mask, arriving, loss_grad, w_first, w_second):
    ticks, images, height, width = act_in.shape[1:5]
    sections = lax.axis_size("section")
    is_last = lax.axis_index("section") == sections - 1
    scale = 1.0 / (ticks * images * lax.axis_size("dp"))
    start = jnp.zeros((1,), jnp.int32)
    filter_rows = w_first.shape[1] * lax.axis_size("dp")
    first_pieces = (filter_rows, start, [lax.all_gather(w_first[0], "dp", axis=0, tiled=True)])
    second_pieces = (filter_rows, start, [lax.all_gather(w_second[0], "dp", axis=0, tiled=True)])
    mask, loss, incoming, in_high, in_low, mid_high, mid_low = prepare(
        height, width, line(relu_mask), line(loss_grad), line(arriving), line(act_in), line(act_mid)
    )
    second = correlate(mid_high[0], mid_low[0], incoming, scale)
    pre, *second_parts = conv(incoming, mask[0], width, pieces=second_pieces)
    out, *first_parts = conv(pre, None, height, pieces=first_pieces)
    outs = [out]
    first = correlate(in_high[0], in_low[0], pre, scale)
    for tick in range(1, ticks):
        above = lax.ppermute(outs[-1], "section", [(i, i - 1) for i in range(1, sections)])
        incoming = jnp.where(is_last, loss[tick - 1], above)
        second = correlate(mid_high[tick], mid_low[tick], incoming, scale, second)
        pre = conv(incoming, mask[tick], width, weights=second_parts)
        first = correlate(in_high[tick], in_low[tick], pre, scale, first)
        if tick < ticks - 1:
            outs.append(conv(pre, None, height, weights=first_parts))
    data_grad = last_conv(pre, first_parts, outs, height, width).reshape(act_in.shape)
    second_grad = lax.psum_scatter(second, "dp", scatter_dimension=0, tiled=True)
    first_grad = lax.psum_scatter(first, "dp", scatter_dimension=0, tiled=True)
    return data_grad, first_grad[None], second_grad[None]


def near_phase(chip):
    half = chip.shape[1] // 2
    a, b = chip[:, :half], chip[:, half:]
    return a, b, swap(jnp.stack([a[1], a[3]]), 2), swap(jnp.stack([b[2], b[3]]), 4)


def far_phase(a, b, a_there, b_there):
    a_near, a_far = a[0] + a_there[0], a[2] + a_there[1]
    a_far, b_there = together(a_far, b_there)
    b_near, b_far = b[0] + b_there[0], b[1] + b_there[1]
    return a_near, b_near, swap(a_far, 4), swap(b_far, 2)


def join(a_near, b_near, a_last, b_last):
    return jnp.concatenate([a_near + a_last, b_near + b_last], axis=0)[None]


def far_pieces(x_piece, y_piece):
    half = x_piece.shape[0] // 2
    return swap(x_piece[:half], 4), swap(y_piece[half:], 2)


def local_eight(act_in, act_mid, relu_mask, arriving, loss_grad, w_first, w_second):
    ticks, images, height, width = act_in.shape[1:5]
    channels = act_in.shape[-1]
    filter_rows = TAPS * channels
    sections = lax.axis_size("section")
    is_last = lax.axis_index("section") == sections - 1
    me = lax.axis_index("dp")
    scale = 1.0 / (ticks * images * lax.axis_size("dp"))
    one, two = w_first[0], w_second[0]
    rows = one.shape[0]
    half = rows // 2
    number = jnp.reshape(me, (1,)).astype(jnp.int32)
    x_two, y_two = swap(two, 2), swap(two, 4)
    x_one, y_one = swap(one, 2), swap(one, 4)
    s_two, s_one = swap(two, 1), swap(one, 1)
    mask, loss, incoming, in_high, in_low, mid_high, mid_low = prepare(
        height, width, line(relu_mask), line(loss_grad), line(arriving), line(act_in), line(act_mid)
    )
    mask, loss, incoming, x_two, y_two, in_high, in_low, mid_high, mid_low = together(
        mask, loss, incoming, x_two, y_two, in_high, in_low, mid_high, mid_low
    )
    ya_two, xb_two = far_pieces(x_two, y_two)
    sx_two, sy_two = swap(x_two, 1), swap(y_two, 1)
    come = [(two, 0, 0), (s_two, 1, 0), (x_two, 2, 0), (y_two, 4, 0), (sx_two, 3, 0), (sy_two, 5, 0)]
    second_parts = placed(*starts_of(me, rows, rows, come), filter_rows)
    ya_one, xb_one = far_pieces(x_one, y_one)
    sx_one, sy_one = swap(x_one, 1), swap(y_one, 1)
    sya_two, sxb_two = swap(ya_two, 1), swap(xb_two, 1)
    come = [(ya_two, 6, 0), (xb_two, 6, half), (sya_two, 7, 0), (sxb_two, 7, half)]
    pre, *second_parts = conv(incoming, mask[0], width, weights=second_parts, pieces=starts_of(me, rows, half, come))
    come = [(one, 0, 0), (s_one, 1, 0), (x_one, 2, 0), (y_one, 4, 0), (sx_one, 3, 0), (sy_one, 5, 0)]
    first_parts = placed(*starts_of(me, rows, rows, come), filter_rows)
    ya_one, xb_one, pre = together(ya_one, xb_one, pre)
    come = [(ya_one, 6, 0), (xb_one, 6, half), (swap(ya_one, 1), 7, 0), (swap(xb_one, 1), 7, half)]
    out, *first_parts = conv(pre, None, height, weights=first_parts, pieces=starts_of(me, rows, half, come))
    outs = [out]
    in_high, in_low, pre, _ = together(in_high, in_low, pre, out)
    second, first = correlate_both((mid_high[0], mid_low[0]), incoming, (in_high[0], in_low[0]), pre, scale)
    for tick in range(1, ticks):
        above = lax.ppermute(outs[-1], "section", [(i, i - 1) for i in range(1, sections)])
        above, first, second = together(above, first, second)
        incoming = jnp.where(is_last, loss[tick - 1], above)
        if tick < ticks - 1:
            second = correlate(mid_high[tick], mid_low[tick], incoming, scale, second)
            pre = conv(incoming, mask[tick], width, weights=second_parts)
            first = correlate(in_high[tick], in_low[tick], pre, scale, first)
            outs.append(conv(pre, None, height, weights=first_parts))
    dealt = correlate(mid_high[-1], mid_low[-1], incoming, scale, second, number)
    kept, other = dealt[0], swap(dealt[1], 1)
    pre = conv(incoming, mask[-1], width, weights=second_parts)
    first_dealt = correlate(in_high[-1], in_low[-1], pre, scale, first, number)
    first_kept, first_other = first_dealt[0], swap(first_dealt[1], 1)
    a, b, a_there, b_there = near_phase(kept + other)
    first_a, first_b, first_a_there, first_b_there = near_phase(first_kept + first_other)
    pre, a_there, b_there = together(pre, a_there, b_there)
    last = far_phase(a, b, a_there, b_there)
    data_grad = last_conv(pre, first_parts, outs, height, width)
    first_last = far_phase(first_a, first_b, first_a_there, first_b_there)
    return data_grad.reshape((1, ticks, images, height, width, channels)), join(*first_last), join(*last)


def local(*arguments):
    return (local_eight if lax.axis_size("dp") == 8 else local_any)(*arguments)


def solution(mesh):
    return jax.shard_map(
        local,
        mesh=mesh,
        in_specs=(
            P("section", None, "dp", None, None, None),
            P("section", None, "dp", None, None, None),
            P("section", None, "dp", None, None, None),
            P("section", "dp", None, None, None),
            P(None, "dp", None, None, None),
            P("section", "dp", None),
            P("section", "dp", None),
        ),
        out_specs=(
            P("section", None, "dp", None, None, None),
            P("section", "dp", None),
            P("section", "dp", None),
        ),
        check_vma=False,
    )
```

```python
import functools

import jax
import jax.numpy as jnp
from jax import lax
from jax.experimental import pallas as pl
from jax.experimental.pallas import tpu as pltpu
from jax.sharding import PartitionSpec as P

TAPS = 7
REACH = TAPS // 2
GROUP = 16
LANES = 128
F32 = jnp.float32
BF16 = jnp.bfloat16
NT = (((1,), (1,)), ((), ()))
NN = (((1,), (0,)), ((), ()))
VMEM = pl.BlockSpec(memory_space=pltpu.VMEM)
SMEM = pl.BlockSpec(memory_space=pltpu.SMEM)
HBM = pl.BlockSpec(memory_space=pltpu.HBM)


def call(kernel, out_shapes, scratch, flops, *operands, scalars=0, aliases=None, far=False, vmem=12):
    moved = sum(x.size * x.dtype.itemsize for x in operands)
    moved += sum(s.size * s.dtype.itemsize for s in out_shapes)
    return pl.pallas_call(
        kernel,
        out_shape=out_shapes,
        in_specs=[SMEM] * scalars + [HBM if far else VMEM] * (len(operands) - scalars),
        out_specs=[VMEM] * len(out_shapes),
        scratch_shapes=scratch,
        input_output_aliases=aliases or {},
        compiler_params=pltpu.CompilerParams(vmem_limit_bytes=vmem * 1024 * 1024),
        cost_estimate=pl.CostEstimate(flops=flops, bytes_accessed=moved, transcendentals=0),
    )(*operands)


def split(value):
    high = value.astype(BF16)
    return high, (value - high.astype(F32)).astype(BF16)


def padded_rows(rows):
    return rows + 2 * REACH * GROUP


def fill(rows_ref, high_ref, low_ref):
    rows, channels = rows_ref.shape
    edge = REACH * GROUP
    border = jnp.zeros((edge, channels), BF16)
    high, low = split(rows_ref[...])
    for ref, body in ((high_ref, high), (low_ref, low)):
        ref[pl.ds(0, edge), :] = border
        ref[pl.ds(edge, rows), :] = body
        ref[pl.ds(edge + rows, edge), :] = border


def dot(a, b, dims):
    return lax.dot_general(a, b, dims, preferred_element_type=F32)


def window(ref, tap, rows):
    return ref[pl.ds((TAPS - 1 - tap) * GROUP, rows), :]


def convolve(high_ref, low_ref, w_high, w_low, rows, columns):
    channels = w_high.shape[0] // TAPS
    width = columns[1] - columns[0]
    total = jnp.zeros((rows, width), F32)
    for tap in range(TAPS):
        taken = pl.ds(tap * channels + columns[0], width)
        high, low = window(high_ref, tap, rows), window(low_ref, tap, rows)
        total += dot(high, w_high[taken, :], NT)
        total += dot(low, w_high[taken, :], NT)
        total += dot(high, w_low[taken, :], NT)
    return total


def regroup(source_ref, out_ref, groups, members):
    tail = jnp.zeros((GROUP - groups, out_ref.shape[-1]), F32)
    for member in range(members):
        for lane in range(source_ref.shape[0]):
            taken = source_ref[lane, pl.ds(member, groups, stride=GROUP), :]
            out_ref[pl.ds(member * GROUP, groups), lane * LANES : (lane + 1) * LANES] = taken
        out_ref[pl.ds(member * GROUP + groups, GROUP - groups), :] = tail


def place(starts_ref, granule, pieces, w_high, w_low):
    index = 0
    for piece in pieces:
        for begin in range(0, piece.shape[0], granule):
            high, low = split(piece[pl.ds(begin, granule), :])
            taken = pl.ds(pl.multiple_of(starts_ref[index], GROUP), granule)
            w_high[taken, :] = high
            w_low[taken, :] = low
            index += 1


def place_kernel(granule, starts_ref, *refs):
    place(starts_ref, granule, refs[:-2], *refs[-2:])


def placed(granule, starts, pieces, filter_rows):
    out = [jax.ShapeDtypeStruct((filter_rows, pieces[0].shape[1]), BF16)] * 2
    return call(functools.partial(place_kernel, granule), out, [], 0, starts, *pieces, scalars=1)


def conv_kernel(piece_count, granule, carried, masked, members, columns, *refs):
    refs = list(refs)
    starts = refs.pop(0) if piece_count else None
    rows_ref = refs.pop(0)
    mask_ref = refs.pop(0) if masked else None
    pieces = [refs.pop(0) for _ in range(piece_count)]
    if carried:
        w_high, w_low = refs.pop(0), refs.pop(0)
    out_ref = refs.pop(0)
    if piece_count:
        w_high, w_low = refs.pop(0), refs.pop(0)
        place(starts, granule, pieces, w_high, w_low)
    high, low, flat = refs
    rows = rows_ref.shape[0]
    fill(rows_ref, high, low)
    total = convolve(high, low, w_high, w_low, rows, columns)
    if masked:
        total = total * mask_ref[...].astype(F32)
    for lane in range(flat.shape[0]):
        flat[lane] = total[:, lane * LANES : (lane + 1) * LANES]
    regroup(flat, out_ref, rows // GROUP, members)


def conv(rows, mask, members, weights=None, pieces=None, columns=None):
    count, channels = rows.shape
    filter_rows = TAPS * channels
    columns = columns or (0, channels)
    width = columns[1] - columns[0]
    granule, starts, parts = pieces or (0, None, [])
    operands = [rows] + ([] if mask is None else [mask]) + parts + list(weights or [])
    out = [jax.ShapeDtypeStruct((members * GROUP, width), F32)]
    aliases = {}
    if parts:
        operands = [starts] + operands
        out += [jax.ShapeDtypeStruct((filter_rows, channels), BF16)] * 2
        if weights:
            aliases = {len(operands) - 2: 1, len(operands) - 1: 2}
    scratch = [
        pltpu.VMEM((padded_rows(count), channels), BF16),
        pltpu.VMEM((padded_rows(count), channels), BF16),
        pltpu.VMEM((width // LANES, count, LANES), F32),
    ]
    kernel = functools.partial(
        conv_kernel, len(parts), granule, bool(weights), mask is not None, members, columns
    )
    flops = 6 * count * filter_rows * width
    result = call(kernel, out, scratch, flops, *operands, scalars=1 if parts else 0, aliases=aliases)
    return result if parts else result[0]


def spread(line_ref, start, height, width, out_ref):
    tail = jnp.zeros((GROUP - width, out_ref.shape[-1]), line_ref.dtype)
    for row in range(height):
        taken = jnp.concatenate([line_ref[pl.ds(start + row * width, width), 0, :], tail])
        out_ref[pl.ds(row * GROUP, GROUP), :] = taken.astype(out_ref.dtype)


def prepare_kernel(height, width, *refs):
    sources, refs = refs[:5], refs[5:]
    row_outs, turned_outs, refs = refs[:3], refs[3:7], refs[7:]
    lines, (flat, grouped, scratch, arrived) = refs[:5], refs[5:]
    copies = [pltpu.make_async_copy(source, held, arrived.at[index]) for index, (source, held) in enumerate(zip(sources, lines))]
    for copy in copies:
        copy.start()
    for copy, held, out in zip(copies, lines, row_outs):
        copy.wait()
        for index in range(out.shape[0]):
            spread(held, index * height * width, height, width, out.at[index])
    in_line, mid_line = lines[3:]
    copies[3].wait()
    copies[4].wait()
    for tick in range(turned_outs[0].shape[0]):
        start = tick * height * width
        spread(in_line, start, height, width, scratch)
        for lane in range(flat.shape[0]):
            flat[lane] = scratch[:, lane * LANES : (lane + 1) * LANES]
        regroup(flat, grouped, height, width)
        turned_outs[0][tick], turned_outs[1][tick] = split(grouped[...].T)
        spread(mid_line, start, height, width, scratch)
        turned_outs[2][tick], turned_outs[3][tick] = split(scratch[...].T)


def prepare(height, width, mask, loss, came, act_in, act_mid):
    sources = [came, mask, loss, act_in, act_mid]
    ticks, channels = act_in.shape[0] // (height * width), act_in.shape[2]
    out = [jax.ShapeDtypeStruct((x.shape[0] // (height * width), height * GROUP, channels), x.dtype) for x in sources[:3]]
    out[1] = jax.ShapeDtypeStruct(out[1].shape, BF16)
    out += [jax.ShapeDtypeStruct((ticks, channels, width * GROUP), BF16)] * 2
    out += [jax.ShapeDtypeStruct((ticks, channels, height * GROUP), BF16)] * 2
    scratch = [pltpu.VMEM(x.shape, x.dtype) for x in sources]
    scratch += [
        pltpu.VMEM((channels // LANES, height * GROUP, LANES), F32),
        pltpu.VMEM((width * GROUP, channels), F32),
        pltpu.VMEM((height * GROUP, channels), F32),
        pltpu.SemaphoreType.DMA((len(sources),)),
    ]
    kernel = functools.partial(prepare_kernel, height, width)
    came, mask, loss, *parts = call(kernel, out, scratch, 0, *sources, far=True, vmem=60)
    return mask, loss, came[0], *parts


def last_kernel(height, width, *refs):
    rows_ref, w_high, w_low = refs[:3]
    before, (line_ref, high, low, flat) = refs[3:-4], refs[-4:]
    for tick, ref in enumerate(before):
        for row in range(height):
            start = (tick * height + row) * width
            line_ref[pl.ds(start, width), 0, :] = ref[pl.ds(row * GROUP, width), :]
    rows = rows_ref.shape[0]
    fill(rows_ref, high, low)
    total = convolve(high, low, w_high, w_low, rows, (0, rows_ref.shape[1]))
    lanes = flat.shape[0]
    for lane in range(lanes):
        flat[lane] = total[:, lane * LANES : (lane + 1) * LANES]
    for row in range(height):
        start = (len(before) * height + row) * width
        taken = [flat[lane, pl.ds(row, width, stride=GROUP), :] for lane in range(lanes)]
        line_ref[pl.ds(start, width), 0, :] = jnp.concatenate(taken, axis=1)


def last_conv(rows, weights, before, height, width):
    count, channels = rows.shape
    out = [jax.ShapeDtypeStruct(((len(before) + 1) * height * width, 1, channels), F32)]
    scratch = [
        pltpu.VMEM((padded_rows(count), channels), BF16),
        pltpu.VMEM((padded_rows(count), channels), BF16),
        pltpu.VMEM((channels // LANES, count, LANES), F32),
    ]
    flops = 6 * count * TAPS * channels * channels
    kernel = functools.partial(last_kernel, height, width)
    return call(kernel, out, scratch, flops, rows, *weights, *before)[0]


def correlate_kernel(scale, carried, dealt, *refs):
    refs = list(refs)
    starts = refs.pop(0) if dealt else None
    act_high, act_low, rows_ref = refs[:3]
    before = refs[3] if carried else None
    out_ref, high, low = refs[3 + carried :]
    fill(rows_ref, high, low)
    rows, channels = rows_ref.shape
    for tap in range(TAPS):
        taken = pl.ds(tap * channels, channels)
        here_high, here_low = window(high, tap, rows), window(low, tap, rows)
        total = dot(act_high[...], here_high, NN)
        total += dot(act_low[...], here_high, NN)
        total += dot(act_high[...], here_low, NN)
        total *= scale
        if carried:
            total += before[taken, :]
        if not dealt:
            out_ref[taken, :] = total
            continue
        block_rows = out_ref.shape[2]
        begin, end = tap * channels, (tap + 1) * channels
        for block in range(begin // block_rows, -(-end // block_rows)):
            first, last = max(begin, block * block_rows), min(end, (block + 1) * block_rows)
            into = pl.ds(first - block * block_rows, last - first)
            distance = jnp.bitwise_xor(block, starts[0])
            place_at = (jnp.bitwise_and(distance, 1), jnp.right_shift(distance, 1), into)
            out_ref[place_at] = total[first - begin : last - begin, :]


def correlate(act_high, act_low, rows, scale, before=None, starts=None):
    count, channels = rows.shape
    filter_rows = TAPS * channels
    scratch = [pltpu.VMEM((padded_rows(count), channels), BF16)] * 2
    operands = [act_high, act_low, rows] + ([] if before is None else [before])
    if starts is None:
        out = [jax.ShapeDtypeStruct((filter_rows, channels), F32)]
    else:
        out = [jax.ShapeDtypeStruct((2, 4, filter_rows // 8, channels), F32)]
        operands = [starts] + operands
    kernel = functools.partial(correlate_kernel, scale, before is not None, starts is not None)
    flops = 6 * count * filter_rows * channels
    result = call(kernel, out, scratch, flops, *operands, scalars=0 if starts is None else 1)
    return result[0]


def both_kernel(scale, *refs):
    two, one, (second_ref, first_ref, high, low) = refs[:3], refs[3:6], refs[6:]
    correlate_kernel(scale, False, False, *two, second_ref, high, low)
    correlate_kernel(scale, False, False, *one, first_ref, high, low)


def correlate_both(mid_parts, incoming, in_parts, pre, scale):
    count, channels = incoming.shape
    out = [jax.ShapeDtypeStruct((TAPS * channels, channels), F32)] * 2
    scratch = [pltpu.VMEM((padded_rows(count), channels), BF16)] * 2
    operands = [*mid_parts, incoming, *in_parts, pre]
    flops = 12 * count * TAPS * channels * channels
    return call(functools.partial(both_kernel, scale), out, scratch, flops, *operands)


def line(values):
    return values.reshape(-1, 1, values.shape[-1])


def swap(shard, bit):
    peers = lax.axis_size("dp")
    return lax.ppermute(shard, "dp", [(i, i ^ bit) for i in range(peers)])


def together(*values):
    return lax.optimization_barrier(values)


def starts_of(me, rows, granule, pieces):
    starts = []
    for piece, bits, offset in pieces:
        bits = bits if isinstance(bits, tuple) else (bits,)
        for begin in range(0, piece.shape[0], granule):
            block = me ^ bits[begin // rows]
            starts.append(block * rows + offset + begin % rows)
    return granule, jnp.stack(starts).astype(jnp.int32), [piece for piece, _, _ in pieces]


def local_any(act_in, act_mid, relu_mask, arriving, loss_grad, w_first, w_second):
    ticks, images, height, width = act_in.shape[1:5]
    sections = lax.axis_size("section")
    is_last = lax.axis_index("section") == sections - 1
    scale = 1.0 / (ticks * images * lax.axis_size("dp"))
    start = jnp.zeros((1,), jnp.int32)
    filter_rows = w_first.shape[1] * lax.axis_size("dp")
    first_pieces = (filter_rows, start, [lax.all_gather(w_first[0], "dp", axis=0, tiled=True)])
    second_pieces = (filter_rows, start, [lax.all_gather(w_second[0], "dp", axis=0, tiled=True)])
    mask, loss, incoming, in_high, in_low, mid_high, mid_low = prepare(
        height, width, line(relu_mask), line(loss_grad), line(arriving), line(act_in), line(act_mid)
    )
    second = correlate(mid_high[0], mid_low[0], incoming, scale)
    pre, *second_parts = conv(incoming, mask[0], width, pieces=second_pieces)
    out, *first_parts = conv(pre, None, height, pieces=first_pieces)
    outs = [out]
    first = correlate(in_high[0], in_low[0], pre, scale)
    for tick in range(1, ticks):
        above = lax.ppermute(outs[-1], "section", [(i, i - 1) for i in range(1, sections)])
        incoming = jnp.where(is_last, loss[tick - 1], above)
        second = correlate(mid_high[tick], mid_low[tick], incoming, scale, second)
        pre = conv(incoming, mask[tick], width, weights=second_parts)
        first = correlate(in_high[tick], in_low[tick], pre, scale, first)
        if tick < ticks - 1:
            outs.append(conv(pre, None, height, weights=first_parts))
    data_grad = last_conv(pre, first_parts, outs, height, width).reshape(act_in.shape)
    second_grad = lax.psum_scatter(second, "dp", scatter_dimension=0, tiled=True)
    first_grad = lax.psum_scatter(first, "dp", scatter_dimension=0, tiled=True)
    return data_grad, first_grad[None], second_grad[None]


def near_phase(chip):
    half = chip.shape[1] // 2
    a, b = chip[:, :half], chip[:, half:]
    return a, b, swap(jnp.stack([a[1], a[3]]), 2), swap(jnp.stack([b[2], b[3]]), 4)


def far_phase(a, b, a_there, b_there):
    a_near, a_far = a[0] + a_there[0], a[2] + a_there[1]
    a_far, b_there = together(a_far, b_there)
    b_near, b_far = b[0] + b_there[0], b[1] + b_there[1]
    return a_near, b_near, swap(a_far, 4), swap(b_far, 2)


def join(a_near, b_near, a_last, b_last):
    return jnp.concatenate([a_near + a_last, b_near + b_last], axis=0)[None]


def far_pieces(x_piece, y_piece):
    half = x_piece.shape[0] // 2
    return swap(x_piece[:half], 4), swap(y_piece[half:], 2)


def local_eight(act_in, act_mid, relu_mask, arriving, loss_grad, w_first, w_second):
    ticks, images, height, width = act_in.shape[1:5]
    channels = act_in.shape[-1]
    filter_rows = TAPS * channels
    sections = lax.axis_size("section")
    is_last = lax.axis_index("section") == sections - 1
    me = lax.axis_index("dp")
    scale = 1.0 / (ticks * images * lax.axis_size("dp"))
    one, two = w_first[0], w_second[0]
    rows = one.shape[0]
    half = rows // 2
    number = jnp.reshape(me, (1,)).astype(jnp.int32)
    x_two, y_two = swap(two, 2), swap(two, 4)
    x_one, y_one = swap(one, 2), swap(one, 4)
    s_two, s_one = swap(two, 1), swap(one, 1)
    mask, loss, incoming, in_high, in_low, mid_high, mid_low = prepare(
        height, width, line(relu_mask), line(loss_grad), line(arriving), line(act_in), line(act_mid)
    )
    mask, loss, incoming, x_two, y_two, in_high, in_low, mid_high, mid_low = together(
        mask, loss, incoming, x_two, y_two, in_high, in_low, mid_high, mid_low
    )
    ya_two, xb_two = far_pieces(x_two, y_two)
    sx_two, sy_two = swap(x_two, 1), swap(y_two, 1)
    come = [(two, 0, 0), (s_two, 1, 0), (x_two, 2, 0), (y_two, 4, 0), (sx_two, 3, 0), (sy_two, 5, 0)]
    second_parts = placed(*starts_of(me, rows, rows, come), filter_rows)
    ya_one, xb_one = far_pieces(x_one, y_one)
    sx_one, sy_one = swap(x_one, 1), swap(y_one, 1)
    sya_two, sxb_two = swap(ya_two, 1), swap(xb_two, 1)
    come = [(ya_two, 6, 0), (xb_two, 6, half), (sya_two, 7, 0), (sxb_two, 7, half)]
    pre, *second_parts = conv(incoming, mask[0], width, weights=second_parts, pieces=starts_of(me, rows, half, come))
    ya_one, xb_one, pre = together(ya_one, xb_one, pre)
    come = [(one, 0, 0), (s_one, 1, 0), (x_one, 2, 0), (y_one, 4, 0), (sx_one, 3, 0), (sy_one, 5, 0)]
    come += [(ya_one, 6, 0), (xb_one, 6, half)]
    first_parts = placed(*starts_of(me, rows, half, come), filter_rows)
    come = [(swap(ya_one, 1), 7, 0), (swap(xb_one, 1), 7, half)]
    out, *first_parts = conv(pre, None, height, weights=first_parts, pieces=starts_of(me, rows, half, come))
    outs = [out]
    in_high, in_low, pre, _ = together(in_high, in_low, pre, out)
    second, first = correlate_both((mid_high[0], mid_low[0]), incoming, (in_high[0], in_low[0]), pre, scale)
    for tick in range(1, ticks):
        above = lax.ppermute(outs[-1], "section", [(i, i - 1) for i in range(1, sections)])
        above, first, second = together(above, first, second)
        incoming = jnp.where(is_last, loss[tick - 1], above)
        if tick < ticks - 1:
            second = correlate(mid_high[tick], mid_low[tick], incoming, scale, second)
            pre = conv(incoming, mask[tick], width, weights=second_parts)
            first = correlate(in_high[tick], in_low[tick], pre, scale, first)
            outs.append(conv(pre, None, height, weights=first_parts))
    dealt = correlate(mid_high[-1], mid_low[-1], incoming, scale, second, number)
    kept, other = dealt[0], swap(dealt[1], 1)
    pre = conv(incoming, mask[-1], width, weights=second_parts)
    first_dealt = correlate(in_high[-1], in_low[-1], pre, scale, first, number)
    first_kept, first_other = first_dealt[0], swap(first_dealt[1], 1)
    a, b, a_there, b_there = near_phase(kept + other)
    first_a, first_b, first_a_there, first_b_there = near_phase(first_kept + first_other)
    pre, a_there, b_there = together(pre, a_there, b_there)
    last = far_phase(a, b, a_there, b_there)
    data_grad = last_conv(pre, first_parts, outs, height, width)
    first_last = far_phase(first_a, first_b, first_a_there, first_b_there)
    return data_grad.reshape((1, ticks, images, height, width, channels)), join(*first_last), join(*last)


def local(*arguments):
    return (local_eight if lax.axis_size("dp") == 8 else local_any)(*arguments)


def solution(mesh):
    return jax.shard_map(
        local,
        mesh=mesh,
        in_specs=(
            P("section", None, "dp", None, None, None),
            P("section", None, "dp", None, None, None),
            P("section", None, "dp", None, None, None),
            P("section", "dp", None, None, None),
            P(None, "dp", None, None, None),
            P("section", "dp", None),
            P("section", "dp", None),
        ),
        out_specs=(
            P("section", None, "dp", None, None, None),
            P("section", "dp", None),
            P("section", "dp", None),
        ),
        check_vma=False,
    )
```

```python
import functools

import jax
import jax.numpy as jnp
from jax import lax
from jax.experimental import pallas as pl
from jax.experimental.pallas import tpu as pltpu
from jax.sharding import PartitionSpec as P

TAPS = 7
REACH = TAPS // 2
GROUP = 16
LANES = 128
F32 = jnp.float32
BF16 = jnp.bfloat16
NT = (((1,), (1,)), ((), ()))
NN = (((1,), (0,)), ((), ()))
VMEM = pl.BlockSpec(memory_space=pltpu.VMEM)
SMEM = pl.BlockSpec(memory_space=pltpu.SMEM)
HBM = pl.BlockSpec(memory_space=pltpu.HBM)


def call(kernel, out_shapes, scratch, flops, *operands, scalars=0, aliases=None, far=False, vmem=12):
    moved = sum(x.size * x.dtype.itemsize for x in operands)
    moved += sum(s.size * s.dtype.itemsize for s in out_shapes)
    return pl.pallas_call(
        kernel,
        out_shape=out_shapes,
        in_specs=[SMEM] * scalars + [HBM if far else VMEM] * (len(operands) - scalars),
        out_specs=[VMEM] * len(out_shapes),
        scratch_shapes=scratch,
        input_output_aliases=aliases or {},
        compiler_params=pltpu.CompilerParams(vmem_limit_bytes=vmem * 1024 * 1024),
        cost_estimate=pl.CostEstimate(flops=flops, bytes_accessed=moved, transcendentals=0),
    )(*operands)


def split(value):
    high = value.astype(BF16)
    return high, (value - high.astype(F32)).astype(BF16)


def padded_rows(rows):
    return rows + 2 * REACH * GROUP


def fill(rows_ref, high_ref, low_ref):
    rows, channels = rows_ref.shape
    edge = REACH * GROUP
    border = jnp.zeros((edge, channels), BF16)
    high, low = split(rows_ref[...])
    for ref, body in ((high_ref, high), (low_ref, low)):
        ref[pl.ds(0, edge), :] = border
        ref[pl.ds(edge, rows), :] = body
        ref[pl.ds(edge + rows, edge), :] = border


def dot(a, b, dims):
    return lax.dot_general(a, b, dims, preferred_element_type=F32)


def window(ref, tap, rows):
    return ref[pl.ds((TAPS - 1 - tap) * GROUP, rows), :]


def convolve(high_ref, low_ref, w_high, w_low, rows, columns):
    channels = w_high.shape[0] // TAPS
    width = columns[1] - columns[0]
    total = jnp.zeros((rows, width), F32)
    for tap in range(TAPS):
        taken = pl.ds(tap * channels + columns[0], width)
        high, low = window(high_ref, tap, rows), window(low_ref, tap, rows)
        total += dot(high, w_high[taken, :], NT)
        total += dot(low, w_high[taken, :], NT)
        total += dot(high, w_low[taken, :], NT)
    return total


def regroup(source_ref, out_ref, groups, members):
    tail = jnp.zeros((GROUP - groups, out_ref.shape[-1]), F32)
    for member in range(members):
        for lane in range(source_ref.shape[0]):
            taken = source_ref[lane, pl.ds(member, groups, stride=GROUP), :]
            out_ref[pl.ds(member * GROUP, groups), lane * LANES : (lane + 1) * LANES] = taken
        out_ref[pl.ds(member * GROUP + groups, GROUP - groups), :] = tail


def place(starts_ref, granule, pieces, w_high, w_low):
    index = 0
    for piece in pieces:
        for begin in range(0, piece.shape[0], granule):
            high, low = split(piece[pl.ds(begin, granule), :])
            taken = pl.ds(pl.multiple_of(starts_ref[index], GROUP), granule)
            w_high[taken, :] = high
            w_low[taken, :] = low
            index += 1


def place_kernel(granule, starts_ref, *refs):
    place(starts_ref, granule, refs[:-2], *refs[-2:])


def placed(granule, starts, pieces, filter_rows):
    out = [jax.ShapeDtypeStruct((filter_rows, pieces[0].shape[1]), BF16)] * 2
    return call(functools.partial(place_kernel, granule), out, [], 0, starts, *pieces, scalars=1)


def conv_kernel(piece_count, granule, carried, masked, members, columns, *refs):
    refs = list(refs)
    starts = refs.pop(0) if piece_count else None
    rows_ref = refs.pop(0)
    mask_ref = refs.pop(0) if masked else None
    pieces = [refs.pop(0) for _ in range(piece_count)]
    if carried:
        w_high, w_low = refs.pop(0), refs.pop(0)
    out_ref = refs.pop(0)
    if piece_count:
        w_high, w_low = refs.pop(0), refs.pop(0)
        place(starts, granule, pieces, w_high, w_low)
    high, low, flat = refs
    rows = rows_ref.shape[0]
    fill(rows_ref, high, low)
    total = convolve(high, low, w_high, w_low, rows, columns)
    if masked:
        total = total * mask_ref[...].astype(F32)
    for lane in range(flat.shape[0]):
        flat[lane] = total[:, lane * LANES : (lane + 1) * LANES]
    regroup(flat, out_ref, rows // GROUP, members)


def conv(rows, mask, members, weights=None, pieces=None, columns=None):
    count, channels = rows.shape
    filter_rows = TAPS * channels
    columns = columns or (0, channels)
    width = columns[1] - columns[0]
    granule, starts, parts = pieces or (0, None, [])
    operands = [rows] + ([] if mask is None else [mask]) + parts + list(weights or [])
    out = [jax.ShapeDtypeStruct((members * GROUP, width), F32)]
    aliases = {}
    if parts:
        operands = [starts] + operands
        out += [jax.ShapeDtypeStruct((filter_rows, channels), BF16)] * 2
        if weights:
            aliases = {len(operands) - 2: 1, len(operands) - 1: 2}
    scratch = [
        pltpu.VMEM((padded_rows(count), channels), BF16),
        pltpu.VMEM((padded_rows(count), channels), BF16),
        pltpu.VMEM((width // LANES, count, LANES), F32),
    ]
    kernel = functools.partial(
        conv_kernel, len(parts), granule, bool(weights), mask is not None, members, columns
    )
    flops = 6 * count * filter_rows * width
    result = call(kernel, out, scratch, flops, *operands, scalars=1 if parts else 0, aliases=aliases)
    return result if parts else result[0]


def spread(line_ref, start, height, width, out_ref):
    tail = jnp.zeros((GROUP - width, out_ref.shape[-1]), line_ref.dtype)
    for row in range(height):
        taken = jnp.concatenate([line_ref[pl.ds(start + row * width, width), 0, :], tail])
        out_ref[pl.ds(row * GROUP, GROUP), :] = taken.astype(out_ref.dtype)


def prepare_kernel(height, width, *refs):
    sources, refs = refs[:5], refs[5:]
    row_outs, turned_outs, refs = refs[:3], refs[3:7], refs[7:]
    lines, (flat, grouped, scratch, arrived) = refs[:5], refs[5:]
    copies = [pltpu.make_async_copy(source, held, arrived.at[index]) for index, (source, held) in enumerate(zip(sources, lines))]
    for copy in copies:
        copy.start()
    for copy, held, out in zip(copies, lines, row_outs):
        copy.wait()
        for index in range(out.shape[0]):
            spread(held, index * height * width, height, width, out.at[index])
    in_line, mid_line = lines[3:]
    copies[3].wait()
    copies[4].wait()
    for tick in range(turned_outs[0].shape[0]):
        start = tick * height * width
        spread(in_line, start, height, width, scratch)
        for lane in range(flat.shape[0]):
            flat[lane] = scratch[:, lane * LANES : (lane + 1) * LANES]
        regroup(flat, grouped, height, width)
        turned_outs[0][tick], turned_outs[1][tick] = split(grouped[...].T)
        spread(mid_line, start, height, width, scratch)
        turned_outs[2][tick], turned_outs[3][tick] = split(scratch[...].T)


def prepare(height, width, mask, loss, came, act_in, act_mid):
    sources = [came, mask, loss, act_in, act_mid]
    ticks, channels = act_in.shape[0] // (height * width), act_in.shape[2]
    out = [jax.ShapeDtypeStruct((x.shape[0] // (height * width), height * GROUP, channels), x.dtype) for x in sources[:3]]
    out[1] = jax.ShapeDtypeStruct(out[1].shape, BF16)
    out += [jax.ShapeDtypeStruct((ticks, channels, width * GROUP), BF16)] * 2
    out += [jax.ShapeDtypeStruct((ticks, channels, height * GROUP), BF16)] * 2
    scratch = [pltpu.VMEM(x.shape, x.dtype) for x in sources]
    scratch += [
        pltpu.VMEM((channels // LANES, height * GROUP, LANES), F32),
        pltpu.VMEM((width * GROUP, channels), F32),
        pltpu.VMEM((height * GROUP, channels), F32),
        pltpu.SemaphoreType.DMA((len(sources),)),
    ]
    kernel = functools.partial(prepare_kernel, height, width)
    came, mask, loss, *parts = call(kernel, out, scratch, 0, *sources, far=True, vmem=60)
    return mask, loss, came[0], *parts


def last_kernel(height, width, *refs):
    rows_ref, w_high, w_low = refs[:3]
    before, (line_ref, high, low, flat) = refs[3:-4], refs[-4:]
    for tick, ref in enumerate(before):
        for row in range(height):
            start = (tick * height + row) * width
            line_ref[pl.ds(start, width), 0, :] = ref[pl.ds(row * GROUP, width), :]
    rows = rows_ref.shape[0]
    fill(rows_ref, high, low)
    total = convolve(high, low, w_high, w_low, rows, (0, rows_ref.shape[1]))
    lanes = flat.shape[0]
    for lane in range(lanes):
        flat[lane] = total[:, lane * LANES : (lane + 1) * LANES]
    for row in range(height):
        start = (len(before) * height + row) * width
        taken = [flat[lane, pl.ds(row, width, stride=GROUP), :] for lane in range(lanes)]
        line_ref[pl.ds(start, width), 0, :] = jnp.concatenate(taken, axis=1)


def last_conv(rows, weights, before, height, width):
    count, channels = rows.shape
    out = [jax.ShapeDtypeStruct(((len(before) + 1) * height * width, 1, channels), F32)]
    scratch = [
        pltpu.VMEM((padded_rows(count), channels), BF16),
        pltpu.VMEM((padded_rows(count), channels), BF16),
        pltpu.VMEM((channels // LANES, count, LANES), F32),
    ]
    flops = 6 * count * TAPS * channels * channels
    kernel = functools.partial(last_kernel, height, width)
    return call(kernel, out, scratch, flops, rows, *weights, *before)[0]


def correlate_kernel(scale, carried, dealt, *refs):
    refs = list(refs)
    starts = refs.pop(0) if dealt else None
    act_high, act_low, rows_ref = refs[:3]
    before = refs[3] if carried else None
    out_ref, high, low = refs[3 + carried :]
    fill(rows_ref, high, low)
    rows, channels = rows_ref.shape
    for tap in range(TAPS):
        taken = pl.ds(tap * channels, channels)
        here_high, here_low = window(high, tap, rows), window(low, tap, rows)
        total = dot(act_high[...], here_high, NN)
        total += dot(act_low[...], here_high, NN)
        total += dot(act_high[...], here_low, NN)
        total *= scale
        if carried:
            total += before[taken, :]
        if not dealt:
            out_ref[taken, :] = total
            continue
        block_rows = out_ref.shape[2]
        begin, end = tap * channels, (tap + 1) * channels
        for block in range(begin // block_rows, -(-end // block_rows)):
            first, last = max(begin, block * block_rows), min(end, (block + 1) * block_rows)
            into = pl.ds(first - block * block_rows, last - first)
            distance = jnp.bitwise_xor(block, starts[0])
            place_at = (jnp.bitwise_and(distance, 1), jnp.right_shift(distance, 1), into)
            out_ref[place_at] = total[first - begin : last - begin, :]


def correlate(act_high, act_low, rows, scale, before=None, starts=None):
    count, channels = rows.shape
    filter_rows = TAPS * channels
    scratch = [pltpu.VMEM((padded_rows(count), channels), BF16)] * 2
    operands = [act_high, act_low, rows] + ([] if before is None else [before])
    if starts is None:
        out = [jax.ShapeDtypeStruct((filter_rows, channels), F32)]
    else:
        out = [jax.ShapeDtypeStruct((2, 4, filter_rows // 8, channels), F32)]
        operands = [starts] + operands
    kernel = functools.partial(correlate_kernel, scale, before is not None, starts is not None)
    flops = 6 * count * filter_rows * channels
    result = call(kernel, out, scratch, flops, *operands, scalars=0 if starts is None else 1)
    return result[0]


def both_kernel(scale, *refs):
    two, one, (second_ref, first_ref, high, low) = refs[:3], refs[3:6], refs[6:]
    correlate_kernel(scale, False, False, *two, second_ref, high, low)
    correlate_kernel(scale, False, False, *one, first_ref, high, low)


def correlate_both(mid_parts, incoming, in_parts, pre, scale):
    count, channels = incoming.shape
    out = [jax.ShapeDtypeStruct((TAPS * channels, channels), F32)] * 2
    scratch = [pltpu.VMEM((padded_rows(count), channels), BF16)] * 2
    operands = [*mid_parts, incoming, *in_parts, pre]
    flops = 12 * count * TAPS * channels * channels
    return call(functools.partial(both_kernel, scale), out, scratch, flops, *operands)


def line(values):
    return values.reshape(-1, 1, values.shape[-1])


def swap(shard, bit):
    peers = lax.axis_size("dp")
    return lax.ppermute(shard, "dp", [(i, i ^ bit) for i in range(peers)])


def together(*values):
    return lax.optimization_barrier(values)


def starts_of(me, rows, granule, pieces):
    starts = []
    for piece, bits, offset in pieces:
        bits = bits if isinstance(bits, tuple) else (bits,)
        for begin in range(0, piece.shape[0], granule):
            block = me ^ bits[begin // rows]
            starts.append(block * rows + offset + begin % rows)
    return granule, jnp.stack(starts).astype(jnp.int32), [piece for piece, _, _ in pieces]


def local_any(act_in, act_mid, relu_mask, arriving, loss_grad, w_first, w_second):
    ticks, images, height, width = act_in.shape[1:5]
    sections = lax.axis_size("section")
    is_last = lax.axis_index("section") == sections - 1
    scale = 1.0 / (ticks * images * lax.axis_size("dp"))
    start = jnp.zeros((1,), jnp.int32)
    filter_rows = w_first.shape[1] * lax.axis_size("dp")
    first_pieces = (filter_rows, start, [lax.all_gather(w_first[0], "dp", axis=0, tiled=True)])
    second_pieces = (filter_rows, start, [lax.all_gather(w_second[0], "dp", axis=0, tiled=True)])
    mask, loss, incoming, in_high, in_low, mid_high, mid_low = prepare(
        height, width, line(relu_mask), line(loss_grad), line(arriving), line(act_in), line(act_mid)
    )
    second = correlate(mid_high[0], mid_low[0], incoming, scale)
    pre, *second_parts = conv(incoming, mask[0], width, pieces=second_pieces)
    out, *first_parts = conv(pre, None, height, pieces=first_pieces)
    outs = [out]
    first = correlate(in_high[0], in_low[0], pre, scale)
    for tick in range(1, ticks):
        above = lax.ppermute(outs[-1], "section", [(i, i - 1) for i in range(1, sections)])
        incoming = jnp.where(is_last, loss[tick - 1], above)
        second = correlate(mid_high[tick], mid_low[tick], incoming, scale, second)
        pre = conv(incoming, mask[tick], width, weights=second_parts)
        first = correlate(in_high[tick], in_low[tick], pre, scale, first)
        if tick < ticks - 1:
            outs.append(conv(pre, None, height, weights=first_parts))
    data_grad = last_conv(pre, first_parts, outs, height, width).reshape(act_in.shape)
    second_grad = lax.psum_scatter(second, "dp", scatter_dimension=0, tiled=True)
    first_grad = lax.psum_scatter(first, "dp", scatter_dimension=0, tiled=True)
    return data_grad, first_grad[None], second_grad[None]


def near_phase(chip):
    half = chip.shape[1] // 2
    a, b = chip[:, :half], chip[:, half:]
    return a, b, swap(jnp.stack([a[1], a[3]]), 2), swap(jnp.stack([b[2], b[3]]), 4)


def far_phase(a, b, a_there, b_there, tied):
    a_near, a_far = a[0] + a_there[0], a[2] + a_there[1]
    if tied:
        a_far, b_there = together(a_far, b_there)
    b_near, b_far = b[0] + b_there[0], b[1] + b_there[1]
    return a_near, b_near, swap(a_far, 4), swap(b_far, 2)


def join(a_near, b_near, a_last, b_last):
    return jnp.concatenate([a_near + a_last, b_near + b_last], axis=0)[None]


def far_pieces(x_piece, y_piece):
    half = x_piece.shape[0] // 2
    return swap(x_piece[:half], 4), swap(y_piece[half:], 2)


def local_eight(act_in, act_mid, relu_mask, arriving, loss_grad, w_first, w_second):
    ticks, images, height, width = act_in.shape[1:5]
    channels = act_in.shape[-1]
    filter_rows = TAPS * channels
    sections = lax.axis_size("section")
    is_last = lax.axis_index("section") == sections - 1
    me = lax.axis_index("dp")
    scale = 1.0 / (ticks * images * lax.axis_size("dp"))
    one, two = w_first[0], w_second[0]
    rows = one.shape[0]
    half = rows // 2
    number = jnp.reshape(me, (1,)).astype(jnp.int32)
    x_two, y_two = swap(two, 2), swap(two, 4)
    x_one, y_one = swap(one, 2), swap(one, 4)
    s_two, s_one = swap(two, 1), swap(one, 1)
    mask, loss, incoming, in_high, in_low, mid_high, mid_low = prepare(
        height, width, line(relu_mask), line(loss_grad), line(arriving), line(act_in), line(act_mid)
    )
    mask, loss, incoming, x_two, y_two, in_high, in_low, mid_high, mid_low = together(
        mask, loss, incoming, x_two, y_two, in_high, in_low, mid_high, mid_low
    )
    ya_two, xb_two = far_pieces(x_two, y_two)
    sx_two, sy_two = swap(x_two, 1), swap(y_two, 1)
    come = [(two, 0, 0), (s_two, 1, 0), (x_two, 2, 0), (y_two, 4, 0), (sx_two, 3, 0), (sy_two, 5, 0)]
    second_parts = placed(*starts_of(me, rows, rows, come), filter_rows)
    ya_one, xb_one = far_pieces(x_one, y_one)
    sx_one, sy_one = swap(x_one, 1), swap(y_one, 1)
    sya_two, sxb_two = swap(ya_two, 1), swap(xb_two, 1)
    come = [(ya_two, 6, 0), (xb_two, 6, half), (sya_two, 7, 0), (sxb_two, 7, half)]
    pre, *second_parts = conv(incoming, mask[0], width, weights=second_parts, pieces=starts_of(me, rows, half, come))
    come = [(one, 0, 0), (s_one, 1, 0), (x_one, 2, 0), (y_one, 4, 0), (sx_one, 3, 0), (sy_one, 5, 0)]
    first_parts = placed(*starts_of(me, rows, rows, come), filter_rows)
    ya_one, xb_one, pre = together(ya_one, xb_one, pre)
    come = [(ya_one, 6, 0), (xb_one, 6, half), (swap(ya_one, 1), 7, 0), (swap(xb_one, 1), 7, half)]
    out, *first_parts = conv(pre, None, height, weights=first_parts, pieces=starts_of(me, rows, half, come))
    outs = [out]
    in_high, in_low, pre, _ = together(in_high, in_low, pre, out)
    second, first = correlate_both((mid_high[0], mid_low[0]), incoming, (in_high[0], in_low[0]), pre, scale)
    for tick in range(1, ticks):
        above = lax.ppermute(outs[-1], "section", [(i, i - 1) for i in range(1, sections)])
        above, first, second = together(above, first, second)
        incoming = jnp.where(is_last, loss[tick - 1], above)
        if tick < ticks - 1:
            second = correlate(mid_high[tick], mid_low[tick], incoming, scale, second)
            pre = conv(incoming, mask[tick], width, weights=second_parts)
            first = correlate(in_high[tick], in_low[tick], pre, scale, first)
            outs.append(conv(pre, None, height, weights=first_parts))
    dealt = correlate(mid_high[-1], mid_low[-1], incoming, scale, second, number)
    kept, other = dealt[0], swap(dealt[1], 1)
    pre = conv(incoming, mask[-1], width, weights=second_parts)
    first_dealt = correlate(in_high[-1], in_low[-1], pre, scale, first, number)
    first_kept, first_other = first_dealt[0], swap(first_dealt[1], 1)
    a, b, a_there, b_there = near_phase(kept + other)
    first_a, first_b, first_a_there, first_b_there = near_phase(first_kept + first_other)
    pre, a_there, b_there = together(pre, a_there, b_there)
    last = far_phase(a, b, a_there, b_there, False)
    data_grad = last_conv(pre, first_parts, outs, height, width)
    first_last = far_phase(first_a, first_b, first_a_there, first_b_there, True)
    return data_grad.reshape((1, ticks, images, height, width, channels)), join(*first_last), join(*last)


def local(*arguments):
    return (local_eight if lax.axis_size("dp") == 8 else local_any)(*arguments)


def solution(mesh):
    return jax.shard_map(
        local,
        mesh=mesh,
        in_specs=(
            P("section", None, "dp", None, None, None),
            P("section", None, "dp", None, None, None),
            P("section", None, "dp", None, None, None),
            P("section", "dp", None, None, None),
            P(None, "dp", None, None, None),
            P("section", "dp", None),
            P("section", "dp", None),
        ),
        out_specs=(
            P("section", None, "dp", None, None, None),
            P("section", "dp", None),
            P("section", "dp", None),
        ),
        check_vma=False,
    )
```
